128 devices in a mesh: row: 32 (over z, y, core), feat: 4 (over x).
Axes of the slice: x: 4, y: 4, z: 4, core: 2. Of those that a mesh axis runs over, the one named last changes fastest.
Arguments:
- bins: int32 [256, 131072], P('feat', 'row'), may hold values from 0 to 255
- grad: bfloat16 [131072], P('row'), as said below
- hess: bfloat16 [131072], P('row'), may hold values from 0.019897461 to 0.19921875
- margin: float32 [131072], P('row'), may hold values from -6 to 6
- node_start: int32 [131072], P('row'), may hold values from 0 to 7
- split_feat1: int32 [8], replicated, may hold values from 0 to 255
- split_bin1: int32 [8], replicated, may hold values from 0 to 255
- split_feat2: int32 [16], replicated, may hold values from 0 to 255
- split_bin2: int32 [16], replicated, may hold values from 0 to 255
Outputs:
- gain1: float32 [8, 256, 256], P(None, ('feat', 'row'))
- gain2: float32 [16, 256, 256], P(None, ('feat', 'row'))
- new_margin: float32 [131072], P('row')
The draws below stay inside these ranges and needn't reach their ends.
Inputs may be any that keep to these rules, and one draw needn't show every extreme that they name: `grad`: gradients of one model's loss, one for each row.
All inputs are finite; a program needn't handle non-finite values.
Results may differ from the reference program's by a relative error of at most 0.0003.
Values sent between devices are 32-bit elements; how exact they have to be, the bound alone decides.
A program may use at most 64 MiB of HBM per device.

```python
import math
import jax
import jax.numpy as jnp
from jax import lax

F = 256
B = 256
NODES1 = 8
ROWS = 131072
NODES2 = 16
LEAVES = 32


def shared_bins(key):
    return jax.random.randint(key, (F, ROWS), 0, B, dtype=jnp.int32)


def draw_bins(key, part):
    values = shared_bins(key)
    return values


def draw_grad(key, part):
    values = shared_bins(key)
    key = jax.random.fold_in(key, 5)
    signs = jax.random.randint(jax.random.fold_in(key, 1), (F,), 0, 2, dtype=jnp.int32) * 2 - 1
    score = jnp.sum(jnp.where(values >= B // 2, signs[:, None], 0), axis=0).astype(jnp.float32)
    noise = 0.25 * jax.random.normal(jax.random.fold_in(key, 2), (ROWS,), jnp.float32)
    return (noise + 0.05 * score).astype(jnp.bfloat16)


def place_ends(entries, own_key, least, top_value):
    place = [jax.random.randint(jax.random.fold_in(own_key, axis), (), 0, length) for axis, length in enumerate(entries.shape)]
    longest = entries.shape.index(max(entries.shape))
    next_to = place[:longest] + [(place[longest] + 1) % entries.shape[longest]] + place[longest + 1:]
    return entries.at[tuple(place)].set(least).at[tuple(next_to)].set(top_value)


def steps_of(stream_key, shape, shards, low, top_value):
    def one(dim, parts):
        draws = jax.random.uniform(jax.random.fold_in(jax.random.fold_in(stream_key, 6), dim), (parts,), jnp.float32, low / len(shards), top_value / len(shards))
        return jnp.repeat(jnp.exp(draws), shape[dim] // parts).reshape((-1,) + (1,) * (len(shape) - dim - 1))

    loudness = one(*shards[0])
    for cut in shards[1:]:
        loudness = loudness * one(*cut)
    return loudness


def centred(own_key, shape, deviation, most, split=(), held_as=jnp.bfloat16):
    array = deviation * jax.random.normal(own_key, shape, jnp.float32)
    if split:
        array = array * steps_of(own_key, shape, split, -0.22, 0.18)
    return jnp.clip(array, -most, most).astype(held_as)


def setup_inputs(seed: int = 0) -> dict:
    key_list = jax.random.split(jax.random.key(seed), 10)
    return {
        "bins": draw_bins(jax.random.fold_in(key_list[9], 71), 0),
        "grad": draw_grad(jax.random.fold_in(key_list[9], 71), 0),
        "hess": jnp.clip(jnp.exp(math.log(0.19921875) - 2.3038113 * jax.random.uniform(key_list[2], (ROWS,), jnp.float32) ** steps_of(key_list[2], (ROWS,), ((0, 32),), -0.2, 0.2)), 0.019897461, 0.19921875).astype(jnp.bfloat16),
        "margin": centred(key_list[3], (ROWS,), 1.0, 6.0, ((0, 32),), jnp.float32),
        "node_start": place_ends(jax.random.randint(key_list[4], (ROWS,), 0, NODES1), jax.random.fold_in(key_list[4], 1), 0, NODES1 - 1).astype(jnp.int32),
        "split_feat1": place_ends(jax.random.randint(key_list[5], (NODES1,), 0, F), jax.random.fold_in(key_list[5], 1), 0, F - 1).astype(jnp.int32),
        "split_bin1": place_ends(jax.random.randint(key_list[6], (NODES1,), 0, B), jax.random.fold_in(key_list[6], 1), 0, B - 1).astype(jnp.int32),
        "split_feat2": place_ends(jax.random.randint(key_list[7], (NODES2,), 0, F), jax.random.fold_in(key_list[7], 1), 0, F - 1).astype(jnp.int32),
        "split_bin2": place_ends(jax.random.randint(key_list[8], (NODES2,), 0, B), jax.random.fold_in(key_list[8], 1), 0, B - 1).astype(jnp.int32),
    }


LAMBDA = 1.0
RATE = 0.3


def histograms(bins, grad, hess, node, nodes):
    grad32 = grad.astype(jnp.float32)
    hess32 = hess.astype(jnp.float32)

    def one_feature(column):
        segment = (node * B + column).astype(jnp.int32)
        first = jax.ops.segment_sum(grad32, segment, num_segments=nodes * B)
        second = jax.ops.segment_sum(hess32, segment, num_segments=nodes * B)
        return jnp.stack([first, second], axis=0)

    stacked = lax.map(one_feature, bins)
    return stacked.reshape(F, 2, nodes, B).transpose(1, 2, 0, 3)


def split_gain(hist):
    summed = jnp.cumsum(hist, axis=-1)
    grad_left = summed[0]
    hess_left = summed[1]
    grad_total = summed[0][..., -1:]
    hess_total = summed[1][..., -1:]
    grad_right = grad_total - grad_left
    hess_right = hess_total - hess_left
    return (grad_left * grad_left / (hess_left + LAMBDA) + grad_right * grad_right / (hess_right + LAMBDA)
            - grad_total * grad_total / (hess_total + LAMBDA))


def route(bins, node, feats, cuts):
    column = feats[node]
    picked = jnp.take_along_axis(bins, column[None, :].astype(jnp.int32), axis=0)[0]
    right = (picked > cuts[node]).astype(jnp.int32)
    return (2 * node + right).astype(jnp.int32)


def reference(bins, grad, hess, margin, node_start, split_feat1, split_bin1, split_feat2, split_bin2):
    hist1 = histograms(bins, grad, hess, node_start, NODES1)
    gain1 = split_gain(hist1)
    child = route(bins, node_start, split_feat1, split_bin1)
    hist2 = histograms(bins, grad, hess, child, NODES2)
    gain2 = split_gain(hist2)
    leaf = route(bins, child, split_feat2, split_bin2)
    grad_sum = jax.ops.segment_sum(grad.astype(jnp.float32), leaf, num_segments=LEAVES)
    hess_sum = jax.ops.segment_sum(hess.astype(jnp.float32), leaf, num_segments=LEAVES)
    weight = -RATE * grad_sum / (hess_sum + LAMBDA)
    new_margin = margin + weight[leaf]
    return gain1, gain2, new_margin
```

```python
import jax
import jax.numpy as jnp
from jax import lax
from jax.experimental import pallas as pl
from jax.experimental.pallas import tpu as pltpu
from jax.sharding import PartitionSpec as P

B = 256
NODES1 = 8
NODES2 = 16
LAMBDA = 1.0
RATE = 0.3

SEG = 86
HI = 88
LO = 3
COLS = 2 * NODES2
UNROLL = 8

MESH = pl.DeviceIdType.MESH
NT = (((1,), (1,)), ((), ()))
TN = (((0,), (0,)), ((), ()))
f32 = jnp.float32
bf16 = jnp.bfloat16


def iota(shape, dim):
    return lax.broadcasted_iota(jnp.int32, shape, dim)


def kernel(bins, rows, table, out1, out2, out_margin,
           hi_s, lo_s, w_s, picked_s, dir_s, kept, sent, mate, part1, part2, sums, tri,
           x1, x2, leaf_mate, leaf_in, leaf_out,
           x1_ss, x1_rs, x2_ss, x2_rs, core_ss, core_rs, p1_ss, p1_rs, p2_ss, p2_rs, leaf_ss, leaf_rs):
    features, count = bins.shape
    me = lax.axis_index("row")
    feat = lax.axis_index("feat")
    z, y, c = me // 8, (me // 2) % 4, me % 2

    def inner(d):
        return (((z + d * c) % 4) * 8 + ((y + d * (1 - c)) % 4) * 2 + c, feat)

    def outer(d):
        return (((z + d * (1 - c)) % 4) * 8 + ((y + d * c) % 4) * 2 + c, feat)

    sibling = (z * 8 + y * 2 + (1 - c), feat)

    def across(d):
        return (me, (feat + d) % 4)

    peers = [sibling] + [axis(d) for axis in (inner, outer, across) for d in (1, 2, 3)]
    barrier = pltpu.get_barrier_semaphore()
    for peer in peers:
        pl.semaphore_signal(barrier, inc=1, device_id=peer, device_id_type=MESH)

    def remote(src, dst, ss, rs, peer):
        return pltpu.make_async_remote_copy(
            src_ref=src, dst_ref=dst, send_sem=ss, recv_sem=rs, device_id=peer, device_id_type=MESH)

    local = table[:, 0:1] - feat * features
    select = jnp.where(local == iota((32, features), 1), 1.0, 0.0).astype(bf16)
    values = bins[...].astype(f32)
    picked = lax.dot_general(select, values.astype(bf16), (((1,), (0,)), ((), ())), preferred_element_type=f32)
    above = jnp.where(picked > table[:, 1:2].astype(f32), 1.0, 0.0)
    node = rows[2:3, :]
    first = node == iota((NODES1, count), 0).astype(f32)
    x1[3] = jnp.max(jnp.where(first, above[0:8], 0.0), axis=0, keepdims=True)
    picked_s[...] = above[8:24]
    pl.semaphore_wait(barrier, len(peers))
    route1 = [remote(x1.at[3], x1.at[d - 1], x1_ss.at[d - 1], x1_rs.at[d - 1], across(d)) for d in (1, 2, 3)]
    for copy in route1:
        copy.start()

    lo = jnp.where(values >= 2.0 * SEG, 2.0, jnp.where(values >= 1.0 * SEG, 1.0, 0.0))
    lo_s[...] = lo
    hi_s[...] = values - SEG * lo
    h = iota((HI, B), 0)
    for k in range(LO):
        tri[k] = jnp.where((h + k * SEG <= iota((HI, B), 1)) & (h < SEG), 1.0, 0.0).astype(bf16)
    for copy in route1:
        copy.wait_recv()
    right = x1[0] + x1[1] + x1[2] + x1[3]
    child = jnp.where(right > 0.5, 8.0, 0.0) + node
    member = child == iota((NODES2, count), 0).astype(f32)
    dir_s[1] = child
    w_s[0:16, :] = jnp.where(member, rows[0:1, :], 0.0).astype(bf16)
    w_s[16:32, :] = jnp.where(member, rows[1:2, :], 0.0).astype(bf16)
    x2[3] = jnp.max(jnp.where(member, picked_s[...], 0.0), axis=0, keepdims=True)
    route2 = [remote(x2.at[3], x2.at[d - 1], x2_ss.at[d - 1], x2_rs.at[d - 1], across(d)) for d in (1, 2, 3)]
    for copy in route2:
        copy.start()

    def feature(i, j, q):
        zo = (z + 1 + i * (1 - q) + j * q) % 4
        yo = (y + 1 + j * (1 - q) + i * q) % 4
        return zo * 16 + yo * 4 + q * 2

    hi_slots = iota((HI, count), 0).astype(f32).astype(bf16)

    def histogram(f):
        table_hi = jnp.where(hi_s[pl.ds(f, 1), :].astype(bf16) == hi_slots, bf16(1), bf16(0))
        lo_row = jnp.broadcast_to(lo_s[pl.ds(f, 1), :].astype(bf16), (COLS, count))
        weights = w_s[...]
        terms = jnp.concatenate([jnp.where(lo_row == bf16(k), weights, bf16(0)) for k in range(LO)], 0)
        return lax.dot_general(table_hi, terms, NT, preferred_element_type=f32)

    def core_copy(t):
        return remote(sent.at[t], mate.at[t], core_ss.at[t], core_rs.at[t], sibling)

    def p1_copy(i, j):
        return remote(kept.at[i * 4 + j], part1.at[i * 3 + j], p1_ss.at[i * 3 + j], p1_rs.at[i * 3 + j], inner(j + 1))

    def p2_copy(i):
        return remote(kept.at[i * 4 + 3], part2.at[i], p2_ss.at[i], p2_rs.at[i], outer(i + 1))

    def finish(i, j):
        t = i * 4 + j
        core_copy(t).wait_recv()
        kept[t] += mate[t]

    def pass_on(i, j):
        finish(i, j)
        p1_copy(i, j).start()

    def gather_plane(i):
        finish(i, 3)
        for j in range(3):
            p1_copy(i, j).wait_recv()
        kept[i * 4 + 3] += part1[i * 3] + part1[i * 3 + 1] + part1[i * 3 + 2]

    def leaf_copy(k):
        if k == 0:
            return [remote(sums.at[0], leaf_mate, leaf_ss.at[0], leaf_rs.at[0], sibling)]
        axis, dst = (inner, leaf_in) if k == 1 else (outer, leaf_out)
        return [remote(sums.at[k], dst.at[d - 1], leaf_ss.at[3 * k - 3 + d], leaf_rs.at[3 * k - 3 + d], axis(d)) for d in (1, 2, 3)]

    def leaves_0():
        for copy in route2:
            copy.wait_recv()
        right2 = jnp.where(x2[0] + x2[1] + x2[2] + x2[3] > 0.5, 1.0, 0.0)
        dir_s[0] = right2
        slot = iota((8, count), 0)
        sides = jnp.where(slot == 0, right2, jnp.where(slot == 1, 1.0 - right2, 0.0)).astype(bf16)
        sums[...] = jnp.zeros_like(sums)
        sums[0, :, 0:8] = lax.dot_general(w_s[...], sides, NT, preferred_element_type=f32)
        leaf_copy(0)[0].start()

    def leaves_1():
        leaf_copy(0)[0].wait_recv()
        sums[1] = sums[0] + leaf_mate[...]
        for copy in leaf_copy(1):
            copy.start()

    def leaves_2():
        for copy in leaf_copy(1):
            copy.wait_recv()
        sums[2] = sums[1] + leaf_in[0] + leaf_in[1] + leaf_in[2]
        for copy in leaf_copy(2):
            copy.start()

    def leaves_3():
        for copy in leaf_copy(2):
            copy.wait_recv()
        total = sums[2] + leaf_out[0] + leaf_out[1] + leaf_out[2]
        weight = -RATE * total[0:16] / (total[16:32] + LAMBDA)
        went = dir_s[0] > 0.5
        mine = dir_s[1] == iota((NODES2, count), 0).astype(f32)
        pick = jnp.where(went, weight[:, 0:1], weight[:, 1:2])
        out_margin[...] = rows[3:4, :] + jnp.sum(jnp.where(mine, pick, 0.0), axis=0, keepdims=True)

    def step(turn, carry):
        i, half = turn // 2, turn % 2
        for s in range(2):
            j = half * 2 + s
            t = i * 4 + j
            for dst, q in ((sent, 1 - c), (kept, c)):
                f = feature(i, j, q)
                for e in range(2):
                    dst[t, e, :, 0:LO * COLS] = histogram(f + e)
        for s in range(2):
            core_copy(i * 4 + half * 2 + s).start()

        @pl.when((turn > 0) & (half == 1))
        def _():
            pass_on(i, 0)
            pass_on(i, 1)

        @pl.when((turn > 0) & (half == 0))
        def _():
            pass_on(i - 1, 2)
            gather_plane(i - 1)
            p2_copy(i - 1).start()

        for k, action in enumerate((leaves_0, leaves_1, leaves_2, leaves_3)):
            pl.when(turn == k + 1)(action)
        return carry

    lax.fori_loop(0, 8, step, 0)
    pass_on(3, 2)
    gather_plane(3)
    for i in range(3):
        p2_copy(i).wait_recv()

    for e in range(2):
        hist = kept[15, e] + part2[0, e] + part2[1, e] + part2[2, e]
        a = hist.astype(bf16)
        rest = hist - a.astype(f32)
        b = rest.astype(bf16)
        d = (rest - b.astype(f32)).astype(bf16)
        total = jnp.zeros((COLS, B), f32)
        for k in range(LO):
            for piece in (d, b, a):
                total += lax.dot_general(piece, tri[k], TN, preferred_element_type=f32)[k * COLS:(k + 1) * COLS]
        g2, h2 = total[0:16], total[16:32]
        for grad_left, hess_left, out, stride in (
            (g2[0:8] + g2[8:16], h2[0:8] + h2[8:16], out1, 1), (g2, h2, out2, 2)):
            grad_total = grad_left[:, B - 1:B]
            hess_total = hess_left[:, B - 1:B]
            grad_right = grad_total - grad_left
            hess_right = hess_total - hess_left
            gain = (grad_left * grad_left / (hess_left + LAMBDA)
                    + grad_right * grad_right / (hess_right + LAMBDA)
                    - grad_total * grad_total / (hess_total + LAMBDA))
            for side in range(stride):
                for n in range(NODES1):
                    out[n * stride + side, e:e + 1, :] = gain[side * 8 + n:side * 8 + n + 1]

    for copy in route1 + route2 + leaf_copy(0) + leaf_copy(1) + leaf_copy(2):
        copy.wait_send()
    for t in range(16):
        core_copy(t).wait_send()
    for i in range(4):
        for j in range(3):
            p1_copy(i, j).wait_send()
    for i in range(3):
        p2_copy(i).wait_send()


def body(bins, grad, hess, margin, node_start, split_feat1, split_bin1, split_feat2, split_bin2):
    features, count = bins.shape
    rows = jnp.stack([grad.astype(f32), hess.astype(f32), node_start.astype(f32), margin])

    def by_side(a):
        return a.reshape(NODES1, 2).T.reshape(NODES2)

    pad = jnp.zeros((8,), jnp.int32)
    table = jnp.stack([
        jnp.concatenate([split_feat1, by_side(split_feat2), pad - 1]),
        jnp.concatenate([split_bin1, by_side(split_bin2), pad])], axis=1)
    own = features * 4 // 128
    dma = pltpu.SemaphoreType.DMA
    pair = (2, HI, 128)
    gain1, gain2, new_margin = pl.pallas_call(
        kernel,
        out_shape=(
            jax.ShapeDtypeStruct((NODES1, own, B), f32),
            jax.ShapeDtypeStruct((NODES2, own, B), f32),
            jax.ShapeDtypeStruct((1, count), f32)),
        in_specs=[pl.BlockSpec(memory_space=pltpu.VMEM)] * 3,
        out_specs=[pl.BlockSpec(memory_space=pltpu.VMEM)] * 3,
        scratch_shapes=[
            pltpu.VMEM((features, count), f32),
            pltpu.VMEM((features, count), f32),
            pltpu.VMEM((COLS, count), bf16),
            pltpu.VMEM((NODES2, count), f32),
            pltpu.VMEM((2, 1, count), f32),
            pltpu.VMEM((16,) + pair, f32),
            pltpu.VMEM((16,) + pair, f32),
            pltpu.VMEM((16,) + pair, f32),
            pltpu.VMEM((12,) + pair, f32),
            pltpu.VMEM((3,) + pair, f32),
            pltpu.VMEM((3, COLS, 128), f32),
            pltpu.VMEM((LO, HI, B), bf16),
            pltpu.VMEM((4, 1, count), f32),
            pltpu.VMEM((4, 1, count), f32),
            pltpu.VMEM((COLS, 128), f32),
            pltpu.VMEM((3, COLS, 128), f32),
            pltpu.VMEM((3, COLS, 128), f32),
            dma((3,)), dma((3,)), dma((3,)), dma((3,)),
            dma((16,)), dma((16,)), dma((12,)), dma((12,)), dma((3,)), dma((3,)),
            dma((7,)), dma((7,)),
        ],
        compiler_params=pltpu.CompilerParams(
            collective_id=0, has_side_effects=True, vmem_limit_bytes=40 * 2**20),
        cost_estimate=pl.CostEstimate(flops=2 * 64 * 4096 * 8192, bytes_accessed=2**20, transcendentals=0),
    )(bins, rows, table)
    return gain1, gain2, new_margin.reshape(count)


def solution(mesh):
    return jax.shard_map(
        body,
        mesh=mesh,
        in_specs=(P("feat", "row"), P("row"), P("row"), P("row"), P("row"), P(), P(), P(), P()),
        out_specs=(P(None, ("feat", "row"), None), P(None, ("feat", "row"), None), P("row")),
        check_vma=False,
    )
```

```python
import jax
import jax.numpy as jnp
from jax import lax
from jax.experimental import pallas as pl
from jax.experimental.pallas import tpu as pltpu
from jax.sharding import PartitionSpec as P

B = 256
NODES1 = 8
NODES2 = 16
LAMBDA = 1.0
RATE = 0.3

SEG = 86
HI = 88
LO = 3
COLS = 2 * NODES2
UNROLL = 8

MESH = pl.DeviceIdType.MESH
NT = (((1,), (1,)), ((), ()))
TN = (((0,), (0,)), ((), ()))
f32 = jnp.float32
bf16 = jnp.bfloat16


def iota(shape, dim):
    return lax.broadcasted_iota(jnp.int32, shape, dim)


def kernel(bins_hbm, grad_hbm, hess_hbm, margin_hbm, node_hbm, feat1, bin1, feat2, bin2, out1, out2, out_margin,
           bins, grad, hess, margin, node_in, packed, in_sem, hi_s, lo_s, w_s, picked_s, dir_s, kept, sent, mate, part1, part2, sums, tri,
           x1, x2, leaf_mate, leaf_in, leaf_out,
           x1_ss, x1_rs, x2_ss, x2_rs, core_ss, core_rs, p1_ss, p1_rs, p2_ss, p2_rs, leaf_ss, leaf_rs):
    features, count = bins.shape
    lines = count // 128
    loads = [pltpu.make_async_copy(src, dst, in_sem.at[k]) for k, (src, dst) in enumerate((
        (bins_hbm, bins), (node_hbm, node_in), (grad_hbm, grad), (hess_hbm, hess), (margin_hbm, margin)))]
    for copy in loads:
        copy.start()

    def row(k):
        return jnp.concatenate([packed[k, r:r + 1, :] for r in range(lines)], axis=1)

    me = lax.axis_index("row")
    feat = lax.axis_index("feat")
    z, y, c = me // 8, (me // 2) % 4, me % 2

    def inner(d):
        return (((z + d * c) % 4) * 8 + ((y + d * (1 - c)) % 4) * 2 + c, feat)

    def outer(d):
        return (((z + d * (1 - c)) % 4) * 8 + ((y + d * c) % 4) * 2 + c, feat)

    def cross(d, q):
        return (((z + d * q) % 4) * 8 + ((y + d * (1 - q)) % 4) * 2 + q, feat)

    sibling = (z * 8 + y * 2 + (1 - c), feat)

    def across(d):
        return (me, (feat + d) % 4)

    peers = [sibling] + [axis(d) for axis in (inner, outer, across) for d in (1, 2, 3)]
    peers.append((((z + c) % 4) * 8 + ((y + 1 - c) % 4) * 2 + 1 - c, feat))
    barrier = pltpu.get_barrier_semaphore()
    for peer in peers:
        pl.semaphore_signal(barrier, inc=1, device_id=peer, device_id_type=MESH)

    def remote(src, dst, ss, rs, peer):
        return pltpu.make_async_remote_copy(
            src_ref=src, dst_ref=dst, send_sem=ss, recv_sem=rs, device_id=peer, device_id_type=MESH)

    line = iota((32, 128), 0)
    owner = jnp.full((32, 128), -1, jnp.int32)
    cut = jnp.zeros((32, 128), jnp.int32)
    for n in range(NODES1):
        owner = jnp.where(line == n, feat1[n], owner)
        cut = jnp.where(line == n, bin1[n], cut)
    for n in range(NODES2):
        at = 8 + (n % 2) * 8 + n // 2
        owner = jnp.where(line == at, feat2[n], owner)
        cut = jnp.where(line == at, bin2[n], cut)
    local = owner - feat * features
    select = jnp.where(local == iota((32, 128), 1), 1.0, 0.0).astype(bf16)[:, 0:features]
    for copy in loads:
        copy.wait()
    packed[0] = grad[...].astype(f32)
    packed[1] = hess[...].astype(f32)
    packed[2] = node_in[...].astype(f32)
    packed[3] = margin[...]
    values = bins[...].astype(f32)
    picked = lax.dot_general(select, values.astype(bf16), (((1,), (0,)), ((), ())), preferred_element_type=f32)
    above = jnp.where(picked > cut[:, 0:1].astype(f32), 1.0, 0.0)
    node = row(2)
    first = node == iota((NODES1, count), 0).astype(f32)
    x1[3] = jnp.max(jnp.where(first, above[0:8], 0.0), axis=0, keepdims=True)
    picked_s[...] = above[8:24]
    pl.semaphore_wait(barrier, len(peers))
    route1 = [remote(x1.at[3], x1.at[d - 1], x1_ss.at[d - 1], x1_rs.at[d - 1], across(d)) for d in (1, 2, 3)]
    for copy in route1:
        copy.start()

    lo = jnp.where(values >= 2.0 * SEG, 2.0, jnp.where(values >= 1.0 * SEG, 1.0, 0.0))
    lo_s[...] = lo
    hi_s[...] = values - SEG * lo
    h = iota((HI, B), 0)
    for k in range(LO):
        tri[k] = jnp.where((h + k * SEG <= iota((HI, B), 1)) & (h < SEG), 1.0, 0.0).astype(bf16)
    for copy in route1:
        copy.wait_recv()
    right = x1[0] + x1[1] + x1[2] + x1[3]
    child = jnp.where(right > 0.5, 8.0, 0.0) + node
    member = child == iota((NODES2, count), 0).astype(f32)
    dir_s[1] = child
    w_s[0:16, :] = jnp.where(member, row(0), 0.0).astype(bf16)
    w_s[16:32, :] = jnp.where(member, row(1), 0.0).astype(bf16)
    x2[3] = jnp.max(jnp.where(member, picked_s[...], 0.0), axis=0, keepdims=True)
    route2 = [remote(x2.at[3], x2.at[d - 1], x2_ss.at[d - 1], x2_rs.at[d - 1], across(d)) for d in (1, 2, 3)]
    for copy in route2:
        copy.start()

    def feature(i, j, q):
        zo = (z + 1 + i * (1 - q) + j * q) % 4
        yo = (y + 1 + j * (1 - q) + i * q) % 4
        return zo * 16 + yo * 4 + q * 2

    hi_slots = iota((HI, count), 0).astype(f32).astype(bf16)

    def histogram(f):
        table_hi = jnp.where(hi_s[pl.ds(f, 1), :].astype(bf16) == hi_slots, bf16(1), bf16(0))
        lo_row = jnp.broadcast_to(lo_s[pl.ds(f, 1), :].astype(bf16), (COLS, count))
        weights = w_s[...]
        terms = jnp.concatenate([jnp.where(lo_row == bf16(k), weights, bf16(0)) for k in range(LO)], 0)
        return lax.dot_general(table_hi, terms, NT, preferred_element_type=f32)

    def core_copy(t):
        return remote(sent.at[t], mate.at[t], core_ss.at[t], core_rs.at[t], sibling)

    def p1_copy(t, slot, j):
        return remote(kept.at[t], part1.at[slot], p1_ss.at[slot], p1_rs.at[slot], inner(j + 1))

    def cross_copy():
        return remote(sent.at[14], part1.at[12], p1_ss.at[12], p1_rs.at[12], cross(3, 1 - c))

    def p2_copy(i):
        return remote(kept.at[9 + i], part2.at[i], p2_ss.at[i], p2_rs.at[i], outer(i + 1))

    def finish(t):
        core_copy(t).wait_recv()
        kept[t] += mate[t]

    def gather_plane(i):
        for j in range(3):
            p1_copy(0, i * 3 + j, j).wait_recv()
        kept[9 + i] += part1[i * 3] + part1[i * 3 + 1] + part1[i * 3 + 2]
        p2_copy(i).start()

    def leaf_copy(k):
        if k == 0:
            return [remote(sums.at[0], leaf_mate, leaf_ss.at[0], leaf_rs.at[0], sibling)]
        axis, dst = (inner, leaf_in) if k == 1 else (outer, leaf_out)
        return [remote(sums.at[k], dst.at[d - 1], leaf_ss.at[3 * k - 3 + d], leaf_rs.at[3 * k - 3 + d], axis(d)) for d in (1, 2, 3)]

    def leaves_0():
        for copy in route2:
            copy.wait_recv()
        right2 = jnp.where(x2[0] + x2[1] + x2[2] + x2[3] > 0.5, 1.0, 0.0)
        dir_s[0] = right2
        slot = iota((8, count), 0)
        sides = jnp.where(slot == 0, right2, jnp.where(slot == 1, 1.0 - right2, 0.0)).astype(bf16)
        sums[...] = jnp.zeros_like(sums)
        sums[0, :, 0:8] = lax.dot_general(w_s[...], sides, NT, preferred_element_type=f32)
        leaf_copy(0)[0].start()

    def leaves_1():
        leaf_copy(0)[0].wait_recv()
        sums[1] = sums[0] + leaf_mate[...]
        for copy in leaf_copy(1):
            copy.start()

    def leaves_2():
        for copy in leaf_copy(1):
            copy.wait_recv()
        sums[2] = sums[1] + leaf_in[0] + leaf_in[1] + leaf_in[2]
        for copy in leaf_copy(2):
            copy.start()

    def leaves_3():
        for copy in leaf_copy(2):
            copy.wait_recv()
        total = sums[2] + leaf_out[0] + leaf_out[1] + leaf_out[2]
        weight = -RATE * total[0:16] / (total[16:32] + LAMBDA)
        went = dir_s[0] > 0.5
        mine = dir_s[1] == iota((NODES2, count), 0).astype(f32)
        pick = jnp.where(went, weight[:, 0:1], weight[:, 1:2])
        result = row(3) + jnp.sum(jnp.where(mine, pick, 0.0), axis=0, keepdims=True)
        for r in range(lines):
            out_margin[r:r + 1, :] = result[:, r * 128:(r + 1) * 128]

    def place(t):
        own = t // 9
        k, r = (t - 9 * own) // 3, (t - 9 * own) % 3
        k0, k1 = (2 - k) // 2, k % 2
        return (1 - own) * k + own * (k0 * r + (1 - k0) * 3), (1 - own) * r + own * (k1 * r + (1 - k1) * 3)

    def step(turn, carry):
        for s in range(2):
            t = turn * 2 + s
            i, j = place(t)
            for dst, q in ((sent, 1 - c), (kept, c)):
                f = feature(i, j, q)
                for e in range(2):
                    dst[t, e, :, 0:LO * COLS] = histogram(f + e)

        @pl.when(turn < 7)
        def _():
            for s in range(2):
                core_copy(turn * 2 + s).start()

        @pl.when((turn > 0) & (turn < 5))
        def _():
            for s in range(2):
                t = turn * 2 - 2 + s
                finish(t)
                p1_copy(t, t, t % 3).start()

        @pl.when(turn == 5)
        def _():
            finish(8)
            p1_copy(8, 8, 2).start()
            finish(9)
            gather_plane(0)

        @pl.when(turn == 6)
        def _():
            finish(10)
            gather_plane(1)
            finish(11)

        @pl.when(turn == 7)
        def _():
            core_copy(15).start()
            p1_copy(14, 11, 2).start()
            cross_copy().start()
            for j in range(2):
                finish(12 + j)
                p1_copy(12 + j, 9 + j, j).start()
            gather_plane(2)

        for k, action in enumerate((leaves_0, leaves_1, leaves_2, leaves_3)):
            pl.when(turn == (1, 2, 4, 6)[k])(action)
        return carry

    lax.fori_loop(0, 8, step, 0)
    finish(15)
    for i in range(3):
        p2_copy(i).wait_recv()
    for j in range(3):
        p1_copy(12 + j, 9 + j, j).wait_recv()
    cross_copy().wait_recv()

    for e in range(2):
        hist = (kept[15, e] + part2[0, e] + part2[1, e] + part2[2, e]
                + part1[9, e] + part1[10, e] + part1[11, e] + part1[12, e])
        a = hist.astype(bf16)
        rest = hist - a.astype(f32)
        b = rest.astype(bf16)
        d = (rest - b.astype(f32)).astype(bf16)
        total = jnp.zeros((COLS, B), f32)
        for k in range(LO):
            for piece in (d, b, a):
                total += lax.dot_general(piece, tri[k], TN, preferred_element_type=f32)[k * COLS:(k + 1) * COLS]
        g2, h2 = total[0:16], total[16:32]
        for grad_left, hess_left, out, stride in (
            (g2[0:8] + g2[8:16], h2[0:8] + h2[8:16], out1, 1), (g2, h2, out2, 2)):
            grad_total = grad_left[:, B - 1:B]
            hess_total = hess_left[:, B - 1:B]
            grad_right = grad_total - grad_left
            hess_right = hess_total - hess_left
            gain = (grad_left * grad_left / (hess_left + LAMBDA)
                    + grad_right * grad_right / (hess_right + LAMBDA)
                    - grad_total * grad_total / (hess_total + LAMBDA))
            for side in range(stride):
                for n in range(NODES1):
                    out[n * stride + side, e:e + 1, :] = gain[side * 8 + n:side * 8 + n + 1]

    for copy in route1 + route2 + leaf_copy(0) + leaf_copy(1) + leaf_copy(2):
        copy.wait_send()
    for t in list(range(14)) + [15]:
        core_copy(t).wait_send()
    for t in list(range(9)) + [12, 13, 14]:
        p1_copy(t, t if t < 9 else t - 3, t % 3).wait_send()
    cross_copy().wait_send()
    for i in range(3):
        p2_copy(i).wait_send()


def copy_kernel(a, b, d, a_out, b_out, d_out):
    for src, dst in ((a, a_out), (b, b_out), (d, d_out)):
        dst[...] = src[...]


def hand_out(*arrays):
    return pl.pallas_call(
        copy_kernel,
        out_shape=tuple(jax.ShapeDtypeStruct(a.shape, a.dtype) for a in arrays),
        in_specs=[pl.BlockSpec(memory_space=pltpu.VMEM)] * 3,
        out_specs=[pl.BlockSpec(memory_space=pltpu.VMEM)] * 3,
        name="hand_out",
    )(*arrays)


def body(bins, grad, hess, margin, node_start, split_feat1, split_bin1, split_feat2, split_bin2):
    features, count = bins.shape
    lines = (count // 128, 128)
    own = features * 4 // 128
    dma = pltpu.SemaphoreType.DMA
    pair = (2, HI, 128)
    gain1, gain2, new_margin = pl.pallas_call(
        kernel,
        out_shape=(
            jax.ShapeDtypeStruct((NODES1, own, B), f32),
            jax.ShapeDtypeStruct((NODES2, own, B), f32),
            jax.ShapeDtypeStruct(lines, f32)),
        in_specs=[pl.BlockSpec(memory_space=pltpu.HBM)] * 5 + [pl.BlockSpec(memory_space=pltpu.SMEM)] * 4,
        out_specs=[pl.BlockSpec(memory_space=pltpu.VMEM)] * 3,
        scratch_shapes=[
            pltpu.VMEM((features, count), jnp.int32),
            pltpu.VMEM(lines, bf16),
            pltpu.VMEM(lines, bf16),
            pltpu.VMEM(lines, f32),
            pltpu.VMEM(lines, jnp.int32),
            pltpu.VMEM((4,) + lines, f32),
            dma((5,)),
            pltpu.VMEM((features, count), f32),
            pltpu.VMEM((features, count), f32),
            pltpu.VMEM((COLS, count), bf16),
            pltpu.VMEM((NODES2, count), f32),
            pltpu.VMEM((2, 1, count), f32),
            pltpu.VMEM((16,) + pair, f32),
            pltpu.VMEM((16,) + pair, f32),
            pltpu.VMEM((16,) + pair, f32),
            pltpu.VMEM((13,) + pair, f32),
            pltpu.VMEM((3,) + pair, f32),
            pltpu.VMEM((3, COLS, 128), f32),
            pltpu.VMEM((LO, HI, B), bf16),
            pltpu.VMEM((4, 1, count), f32),
            pltpu.VMEM((4, 1, count), f32),
            pltpu.VMEM((COLS, 128), f32),
            pltpu.VMEM((3, COLS, 128), f32),
            pltpu.VMEM((3, COLS, 128), f32),
            dma((3,)), dma((3,)), dma((3,)), dma((3,)),
            dma((16,)), dma((16,)), dma((13,)), dma((13,)), dma((3,)), dma((3,)),
            dma((7,)), dma((7,)),
        ],
        compiler_params=pltpu.CompilerParams(
            collective_id=0, has_side_effects=True, vmem_limit_bytes=60 * 2**20),
        cost_estimate=pl.CostEstimate(flops=2 * 64 * 4096 * 8192, bytes_accessed=2**20, transcendentals=0),
    )(bins, grad.reshape(lines), hess.reshape(lines), margin.reshape(lines), node_start.reshape(lines),
      split_feat1, split_bin1, split_feat2, split_bin2)
    gain1, gain2, new_margin = hand_out(gain1, gain2, new_margin)
    return gain1, gain2, new_margin.reshape(count)


def solution(mesh):
    return jax.shard_map(
        body,
        mesh=mesh,
        in_specs=(P("feat", "row"), P("row"), P("row"), P("row"), P("row"), P(), P(), P(), P()),
        out_specs=(P(None, ("feat", "row"), None), P(None, ("feat", "row"), None), P("row")),
        check_vma=False,
    )
```

```python
import jax
import jax.numpy as jnp
from jax import lax
from jax.experimental import pallas as pl
from jax.experimental.pallas import tpu as pltpu
from jax.sharding import PartitionSpec as P

B = 256
NODES1 = 8
NODES2 = 16
LAMBDA = 1.0
RATE = 0.3

SEG = 86
HI = 88
FOLD = 48
LO = 3
COLS = 2 * NODES2
OWN = (9, 10, 12)

MESH = pl.DeviceIdType.MESH
NT = (((1,), (1,)), ((), ()))
TN = (((0,), (0,)), ((), ()))
f32 = jnp.float32
bf16 = jnp.bfloat16


def iota(shape, dim):
    return lax.broadcasted_iota(jnp.int32, shape, dim)


def kernel(bins_hbm, grad_hbm, hess_hbm, margin_hbm, node_hbm, feat1, bin1, feat2, bin2, out1, out2, out_margin,
           bins, grad, hess, margin, node_in, packed, in_sem, hi_s, lo_s, w_s, picked_s, dir_s, kept, sent, mate, part1, part2, sums, tri,
           x1, x2, leaf_mate, leaf_in, leaf_out, wide,
           x1_ss, x1_rs, x2_ss, x2_rs, core_ss, core_rs, p1_ss, p1_rs, p2_ss, p2_rs, leaf_ss, leaf_rs):
    features, count = bins.shape
    lines = count // 128
    loads = [pltpu.make_async_copy(src, dst, in_sem.at[k]) for k, (src, dst) in enumerate((
        (bins_hbm, bins), (node_hbm, node_in), (grad_hbm, grad), (hess_hbm, hess), (margin_hbm, margin)))]
    for copy in loads:
        copy.start()

    def row(k):
        return jnp.concatenate([packed[k, r:r + 1, :] for r in range(lines)], axis=1)

    me = lax.axis_index("row")
    feat = lax.axis_index("feat")
    z, y, c = me // 8, (me // 2) % 4, me % 2

    def inner(d):
        return (((z + d * c) % 4) * 8 + ((y + d * (1 - c)) % 4) * 2 + c, feat)

    def outer(d):
        return (((z + d * (1 - c)) % 4) * 8 + ((y + d * c) % 4) * 2 + c, feat)

    def cross(d, q):
        return (((z + d * q) % 4) * 8 + ((y + d * (1 - q)) % 4) * 2 + q, feat)

    sibling = (z * 8 + y * 2 + (1 - c), feat)

    def across(d):
        return (me, (feat + d) % 4)

    peers = [sibling] + [axis(d) for axis in (inner, outer, across) for d in (1, 2, 3)]
    peers.append((((z + 3 * c) % 4) * 8 + ((y + 3 - 3 * c) % 4) * 2 + 1 - c, feat))
    barrier = pltpu.get_barrier_semaphore()
    for peer in peers:
        pl.semaphore_signal(barrier, inc=1, device_id=peer, device_id_type=MESH)

    def remote(src, dst, ss, rs, peer):
        return pltpu.make_async_remote_copy(
            src_ref=src, dst_ref=dst, send_sem=ss, recv_sem=rs, device_id=peer, device_id_type=MESH)

    line = iota((32, 128), 0)
    owner = jnp.full((32, 128), -1, jnp.int32)
    cut = jnp.zeros((32, 128), jnp.int32)
    for n in range(NODES1):
        owner = jnp.where(line == n, feat1[n], owner)
        cut = jnp.where(line == n, bin1[n], cut)
    for n in range(NODES2):
        at = 8 + (n % 2) * 8 + n // 2
        owner = jnp.where(line == at, feat2[n], owner)
        cut = jnp.where(line == at, bin2[n], cut)
    local = owner - feat * features
    select = jnp.where(local == iota((32, 128), 1), 1.0, 0.0).astype(bf16)[:, 0:features]
    for copy in loads:
        copy.wait()
    packed[0] = grad[...].astype(f32)
    packed[1] = hess[...].astype(f32)
    packed[2] = node_in[...].astype(f32)
    packed[3] = margin[...]
    values = bins[...].astype(f32)
    picked = lax.dot_general(select, values.astype(bf16), (((1,), (0,)), ((), ())), preferred_element_type=f32)
    above = jnp.where(picked > cut[:, 0:1].astype(f32), 1.0, 0.0)
    node = row(2)
    first = node == iota((NODES1, count), 0).astype(f32)
    x1[3] = jnp.max(jnp.where(first, above[0:8], 0.0), axis=0, keepdims=True)
    picked_s[...] = above[8:24]
    pl.semaphore_wait(barrier, len(peers))
    route1 = [remote(x1.at[3], x1.at[d - 1], x1_ss.at[d - 1], x1_rs.at[d - 1], across(d)) for d in (1, 2, 3)]
    for copy in route1:
        copy.start()

    lo = jnp.where(values >= 2.0 * SEG, 2.0, jnp.where(values >= 1.0 * SEG, 1.0, 0.0))
    lo_s[...] = lo
    hi_s[...] = values - SEG * lo
    h = iota((2 * FOLD, B), 0)
    for k in range(LO):
        tri[k] = jnp.where((h + k * SEG <= iota((2 * FOLD, B), 1)) & (h < SEG), 1.0, 0.0).astype(bf16)
    for copy in route1:
        copy.wait_recv()
    right = x1[0] + x1[1] + x1[2] + x1[3]
    child = jnp.where(right > 0.5, 8.0, 0.0) + node
    member = child == iota((NODES2, count), 0).astype(f32)
    dir_s[1] = child
    w_s[0:16, :] = jnp.where(member, row(0), 0.0).astype(bf16)
    w_s[16:32, :] = jnp.where(member, row(1), 0.0).astype(bf16)
    x2[3] = jnp.max(jnp.where(member, picked_s[...], 0.0), axis=0, keepdims=True)
    route2 = [remote(x2.at[3], x2.at[d - 1], x2_ss.at[d - 1], x2_rs.at[d - 1], across(d)) for d in (1, 2, 3)]
    for copy in route2:
        copy.start()

    def feature(i, j, q):
        zo = (z + 1 + i * (1 - q) + j * q) % 4
        yo = (y + 1 + j * (1 - q) + i * q) % 4
        return zo * 16 + yo * 4 + q * 2

    hi_slots = iota((HI, count), 0).astype(f32).astype(bf16)

    def histogram(f):
        table_hi = jnp.where(hi_s[pl.ds(f, 1), :].astype(bf16) == hi_slots, bf16(1), bf16(0))
        lo_row = jnp.broadcast_to(lo_s[pl.ds(f, 1), :].astype(bf16), (COLS, count))
        weights = w_s[...]
        terms = jnp.concatenate([jnp.where(lo_row == bf16(k), weights, bf16(0)) for k in range(LO)], 0)
        return lax.dot_general(table_hi, terms, NT, preferred_element_type=f32)

    def core_copy(t):
        return remote(sent.at[t], mate.at[t], core_ss.at[t], core_rs.at[t], sibling)

    def p1_copy(t, slot, j):
        return remote(kept.at[t], part1.at[slot], p1_ss.at[slot], p1_rs.at[slot], inner(j + 1))

    def cross_copy():
        return remote(sent.at[14], part1.at[12], p1_ss.at[12], p1_rs.at[12], cross(1, 1 - c))

    def p2_copy(i):
        return remote(kept.at[OWN[i]], part2.at[i], p2_ss.at[i], p2_rs.at[i], outer(i + 1))

    def finish(t):
        core_copy(t).wait_recv()
        kept[t] += mate[t]

    def gather_plane(i):
        for j in range(3):
            p1_copy(0, i * 3 + j, j).wait_recv()
        kept[OWN[i]] += part1[i * 3] + part1[i * 3 + 1] + part1[i * 3 + 2]
        p2_copy(i).start()

    def leaf_copy(k):
        if k == 0:
            return [remote(sums.at[0], leaf_mate, leaf_ss.at[0], leaf_rs.at[0], sibling)]
        axis, dst = (inner, leaf_in) if k == 1 else (outer, leaf_out)
        return [remote(sums.at[k], dst.at[d - 1], leaf_ss.at[3 * k - 3 + d], leaf_rs.at[3 * k - 3 + d], axis(d)) for d in (1, 2, 3)]

    def leaves_0():
        for copy in route2:
            copy.wait_recv()
        right2 = jnp.where(x2[0] + x2[1] + x2[2] + x2[3] > 0.5, 1.0, 0.0)
        dir_s[0] = right2
        slot = iota((8, count), 0)
        sides = jnp.where(slot == 0, right2, jnp.where(slot == 1, 1.0 - right2, 0.0)).astype(bf16)
        sums[...] = jnp.zeros_like(sums)
        sums[0, :, 0:8] = lax.dot_general(w_s[...], sides, NT, preferred_element_type=f32)
        leaf_copy(0)[0].start()

    def leaves_1():
        leaf_copy(0)[0].wait_recv()
        sums[1] = sums[0] + leaf_mate[...]
        for copy in leaf_copy(1):
            copy.start()

    def leaves_2():
        for copy in leaf_copy(1):
            copy.wait_recv()
        sums[2] = sums[1] + leaf_in[0] + leaf_in[1] + leaf_in[2]
        for copy in leaf_copy(2):
            copy.start()

    def leaves_3():
        for copy in leaf_copy(2):
            copy.wait_recv()
        total = sums[2] + leaf_out[0] + leaf_out[1] + leaf_out[2]
        weight = -RATE * total[0:16] / (total[16:32] + LAMBDA)
        went = dir_s[0] > 0.5
        mine = dir_s[1] == iota((NODES2, count), 0).astype(f32)
        pick = jnp.where(went, weight[:, 0:1], weight[:, 1:2])
        result = row(3) + jnp.sum(jnp.where(mine, pick, 0.0), axis=0, keepdims=True)
        for r in range(lines):
            out_margin[r:r + 1, :] = result[:, r * 128:(r + 1) * 128]

    def place(t):
        own, v = t // 9, t % 9
        late = v // 4
        mid = (v // 2) * (1 - late)
        at2, at3 = mid * (1 - v % 2), mid * (v % 2)
        i = (1 - own) * (v // 3) + own * (v + at2 - at3 - late)
        j = (1 - own) * (v % 3) + own * (3 - 2 * at2 - late)
        return i, j

    def fill(dst, t, f):
        for e in range(2):
            wide[e, :, 0:LO * COLS] = histogram(f + e)
        one, two = wide[0], wide[1]
        lane = iota((HI, 128), 1)
        dst[t, 0:HI] = jnp.where(lane < LO * COLS, one, pltpu.roll(two, COLS, 1))
        below = jnp.concatenate([two[FOLD:HI], jnp.zeros((2 * FOLD - HI, 128), f32)], 0)
        dst[t, HI:HI + FOLD] = jnp.where(lane[0:FOLD] < 64, two[0:FOLD], pltpu.roll(below, 64, 1))

    def compute_sent(t, i, j):
        fill(sent, t, feature(i, j, 1 - c))

    def compute_kept(t, i, j):
        fill(kept, t, feature(i, j, c))

    def step(turn, carry):
        for s in range(2):
            t = turn * 2 + s
            compute_sent(t, *place(t))
            compute_kept(t, *place(t))
        for s in range(2):
            core_copy(turn * 2 + s).start()

        @pl.when((turn > 0) & (turn < 5))
        def _():
            for s in range(2):
                t = turn * 2 - 2 + s
                finish(t)
                p1_copy(t, t, t % 3).start()

        @pl.when(turn == 5)
        def _():
            finish(8)
            p1_copy(8, 8, 2).start()
            finish(9)
            gather_plane(0)

        @pl.when(turn == 6)
        def _():
            finish(11)
            p1_copy(11, 9, 1).start()
            finish(10)
            gather_plane(1)

        for k, action in enumerate((leaves_0, leaves_1, leaves_2)):
            pl.when(turn == (1, 2, 4)[k])(action)
        return carry

    lax.fori_loop(0, 7, step, 0)
    compute_sent(14, 3, 0)
    cross_copy().start()
    compute_kept(14, 3, 0)
    p1_copy(14, 11, 0).start()
    finish(13)
    p1_copy(13, 10, 2).start()
    finish(12)
    gather_plane(2)
    compute_sent(15, 3, 3)
    core_copy(15).start()
    compute_kept(15, 3, 3)
    leaves_3()
    finish(15)
    for i in range(3):
        p2_copy(i).wait_recv()
    for t, slot, j in ((11, 9, 1), (13, 10, 2), (14, 11, 0)):
        p1_copy(t, slot, j).wait_recv()
    cross_copy().wait_recv()

    hist = (kept[15] + part2[0] + part2[1] + part2[2] + part1[9] + part1[10] + part1[11] + part1[12])

    def split(x):
        a = x.astype(bf16)
        rest = x - a.astype(f32)
        b = rest.astype(bf16)
        return (rest - b.astype(f32)).astype(bf16), b, a

    def summed(pieces, ones):
        return sum(lax.dot_general(piece, ones, TN, preferred_element_type=f32) for piece in pieces)

    upper = split(jnp.concatenate([hist[0:HI], jnp.zeros((2 * FOLD - HI, 128), f32)], 0))
    folded = split(hist[HI:HI + FOLD])
    tops = [summed(upper, tri[k]) for k in range(LO)]
    first_half = [summed(folded, tri[k, 0:FOLD]) for k in range(2)]
    second_half = [summed(folded, tri[k, FOLD:2 * FOLD]) for k in range(2)]
    totals = (tops[0][0:32] + tops[1][32:64] + tops[2][64:96],
              first_half[0][0:32] + second_half[0][64:96] + first_half[1][32:64] + second_half[1][96:128] + tops[2][96:128])
    for e, total in enumerate(totals):
        g2, h2 = total[0:16], total[16:32]
        for grad_left, hess_left, out, stride in (
            (g2[0:8] + g2[8:16], h2[0:8] + h2[8:16], out1, 1), (g2, h2, out2, 2)):
            grad_total = grad_left[:, B - 1:B]
            hess_total = hess_left[:, B - 1:B]
            grad_right = grad_total - grad_left
            hess_right = hess_total - hess_left
            gain = (grad_left * grad_left / (hess_left + LAMBDA)
                    + grad_right * grad_right / (hess_right + LAMBDA)
                    - grad_total * grad_total / (hess_total + LAMBDA))
            for side in range(stride):
                for n in range(NODES1):
                    out[n * stride + side, e:e + 1, :] = gain[side * 8 + n:side * 8 + n + 1]

    for copy in route1 + route2 + leaf_copy(0) + leaf_copy(1) + leaf_copy(2):
        copy.wait_send()
    for t in list(range(14)) + [15]:
        core_copy(t).wait_send()
    for t in range(9):
        p1_copy(t, t, t % 3).wait_send()
    for t, slot, j in ((11, 9, 1), (13, 10, 2), (14, 11, 0)):
        p1_copy(t, slot, j).wait_send()
    cross_copy().wait_send()
    for i in range(3):
        p2_copy(i).wait_send()


def copy_kernel(a, b, d, a_out, b_out, d_out):
    for src, dst in ((a, a_out), (b, b_out), (d, d_out)):
        dst[...] = src[...]


def hand_out(*arrays):
    return pl.pallas_call(
        copy_kernel,
        out_shape=tuple(jax.ShapeDtypeStruct(a.shape, a.dtype) for a in arrays),
        in_specs=[pl.BlockSpec(memory_space=pltpu.VMEM)] * 3,
        out_specs=[pl.BlockSpec(memory_space=pltpu.VMEM)] * 3,
        name="hand_out",
    )(*arrays)


def body(bins, grad, hess, margin, node_start, split_feat1, split_bin1, split_feat2, split_bin2):
    features, count = bins.shape
    lines = (count // 128, 128)
    own = features * 4 // 128
    dma = pltpu.SemaphoreType.DMA
    pair = (HI + FOLD, 128)
    gain1, gain2, new_margin = pl.pallas_call(
        kernel,
        out_shape=(
            jax.ShapeDtypeStruct((NODES1, own, B), f32),
            jax.ShapeDtypeStruct((NODES2, own, B), f32),
            jax.ShapeDtypeStruct(lines, f32)),
        in_specs=[pl.BlockSpec(memory_space=pltpu.HBM)] * 5 + [pl.BlockSpec(memory_space=pltpu.SMEM)] * 4,
        out_specs=[pl.BlockSpec(memory_space=pltpu.VMEM)] * 3,
        scratch_shapes=[
            pltpu.VMEM((features, count), jnp.int32),
            pltpu.VMEM(lines, bf16),
            pltpu.VMEM(lines, bf16),
            pltpu.VMEM(lines, f32),
            pltpu.VMEM(lines, jnp.int32),
            pltpu.VMEM((4,) + lines, f32),
            dma((5,)),
            pltpu.VMEM((features, count), f32),
            pltpu.VMEM((features, count), f32),
            pltpu.VMEM((COLS, count), bf16),
            pltpu.VMEM((NODES2, count), f32),
            pltpu.VMEM((2, 1, count), f32),
            pltpu.VMEM((16,) + pair, f32),
            pltpu.VMEM((16,) + pair, f32),
            pltpu.VMEM((16,) + pair, f32),
            pltpu.VMEM((13,) + pair, f32),
            pltpu.VMEM((3,) + pair, f32),
            pltpu.VMEM((3, COLS, 128), f32),
            pltpu.VMEM((LO, 2 * FOLD, B), bf16),
            pltpu.VMEM((4, 1, count), f32),
            pltpu.VMEM((4, 1, count), f32),
            pltpu.VMEM((COLS, 128), f32),
            pltpu.VMEM((3, COLS, 128), f32),
            pltpu.VMEM((3, COLS, 128), f32),
            pltpu.VMEM((2, HI, 128), f32),
            dma((3,)), dma((3,)), dma((3,)), dma((3,)),
            dma((16,)), dma((16,)), dma((13,)), dma((13,)), dma((3,)), dma((3,)),
            dma((7,)), dma((7,)),
        ],
        compiler_params=pltpu.CompilerParams(
            collective_id=0, has_side_effects=True, vmem_limit_bytes=60 * 2**20),
        cost_estimate=pl.CostEstimate(flops=2 * 64 * 4096 * 8192, bytes_accessed=2**20, transcendentals=0),
    )(bins, grad.reshape(lines), hess.reshape(lines), margin.reshape(lines), node_start.reshape(lines),
      split_feat1, split_bin1, split_feat2, split_bin2)
    gain1, gain2, new_margin = hand_out(gain1, gain2, new_margin)
    return gain1, gain2, new_margin.reshape(count)


def solution(mesh):
    return jax.shard_map(
        body,
        mesh=mesh,
        in_specs=(P("feat", "row"), P("row"), P("row"), P("row"), P("row"), P(), P(), P(), P()),
        out_specs=(P(None, ("feat", "row"), None), P(None, ("feat", "row"), None), P("row")),
        check_vma=False,
    )
```

```python
import jax
import jax.numpy as jnp
from jax import lax
from jax.experimental import pallas as pl
from jax.experimental.pallas import tpu as pltpu
from jax.sharding import PartitionSpec as P

B = 256
NODES1 = 8
NODES2 = 16
LAMBDA = 1.0
RATE = 0.3

SEG = 86
HI = 88
FOLD = 48
LO = 3
COLS = 2 * NODES2
OWN = (9, 10, 12)

MESH = pl.DeviceIdType.MESH
NT = (((1,), (1,)), ((), ()))
TN = (((0,), (0,)), ((), ()))
f32 = jnp.float32
bf16 = jnp.bfloat16


def iota(shape, dim):
    return lax.broadcasted_iota(jnp.int32, shape, dim)


def kernel(bins_hbm, grad_hbm, hess_hbm, margin_hbm, node_hbm, feat1_hbm, bin1_hbm, feat2_hbm, bin2_hbm,
           out1_hbm, out2_hbm, margin_out_hbm,
           bins, grad, hess, margin, node_in, feat1, bin1, feat2, bin2, out1, out2, out_margin,
           packed, first_s, in_sem, out_sem, hi_s, lo_s, w_s, picked_s, dir_s, kept, sent, mate, part1, part2, sums, tri,
           x1, x2, leaf_mate, leaf_in, leaf_out, wide,
           x1_ss, x1_rs, x2_ss, x2_rs, core_ss, core_rs, p1_ss, p1_rs, p2_ss, p2_rs, leaf_ss, leaf_rs):
    features, count = bins.shape
    lines = count // 128
    loads = [pltpu.make_async_copy(src, dst, in_sem.at[k]) for k, (src, dst) in enumerate((
        (bins_hbm, bins), (node_hbm, node_in), (feat1_hbm, feat1), (bin1_hbm, bin1), (feat2_hbm, feat2), (bin2_hbm, bin2),
        (grad_hbm, grad), (hess_hbm, hess), (margin_hbm, margin)))]
    stores = [pltpu.make_async_copy(src, dst, out_sem.at[k]) for k, (src, dst) in enumerate((
        (out1, out1_hbm), (out2, out2_hbm), (out_margin, margin_out_hbm)))]
    for copy in loads:
        copy.start()

    def row(k):
        return jnp.concatenate([packed[k, r:r + 1, :] for r in range(lines)], axis=1)

    me = lax.axis_index("row")
    feat = lax.axis_index("feat")
    z, y, c = me // 8, (me // 2) % 4, me % 2

    def inner(d):
        return (((z + d * c) % 4) * 8 + ((y + d * (1 - c)) % 4) * 2 + c, feat)

    def outer(d):
        return (((z + d * (1 - c)) % 4) * 8 + ((y + d * c) % 4) * 2 + c, feat)

    def cross(d, q):
        return (((z + d * q) % 4) * 8 + ((y + d * (1 - q)) % 4) * 2 + q, feat)

    sibling = (z * 8 + y * 2 + (1 - c), feat)

    def across(d):
        return (me, (feat + d) % 4)

    peers = [sibling] + [axis(d) for axis in (inner, outer, across) for d in (1, 2, 3)]
    peers.append((((z + 3 * c) % 4) * 8 + ((y + 3 - 3 * c) % 4) * 2 + 1 - c, feat))
    barrier = pltpu.get_barrier_semaphore()
    for peer in peers:
        pl.semaphore_signal(barrier, inc=1, device_id=peer, device_id_type=MESH)

    def remote(src, dst, ss, rs, peer):
        return pltpu.make_async_remote_copy(
            src_ref=src, dst_ref=dst, send_sem=ss, recv_sem=rs, device_id=peer, device_id_type=MESH)

    for copy in loads[:4]:
        copy.wait()
    slot8 = iota((NODES1, 128), 0)
    low = jnp.full((NODES1, 128), B, jnp.int32)
    for n in range(NODES1):
        at = feat1[n] - feat * features
        inside = jnp.clip(at, 0, features - 1)
        first_s[n:n + 1, :] = bins[pl.ds(inside, 1), :]
        low = jnp.where((slot8 == n) & (jnp.full((NODES1, 128), at, jnp.int32) == inside), bin1[n], low)
    node_rows = jnp.concatenate([node_in[r:r + 1, :] for r in range(lines)], axis=1)
    taken = (first_s[...] > low[:, 0:1]) & (node_rows == iota((NODES1, count), 0))
    x1[3] = jnp.max(jnp.where(taken, 1.0, 0.0), axis=0, keepdims=True)
    pl.semaphore_wait(barrier, len(peers))
    route1 = [remote(x1.at[3], x1.at[d - 1], x1_ss.at[d - 1], x1_rs.at[d - 1], across(d)) for d in (1, 2, 3)]
    for copy in route1:
        copy.start()

    for copy in loads[4:]:
        copy.wait()
    line = iota((NODES2, 128), 0)
    owner = jnp.full((NODES2, 128), -1, jnp.int32)
    cut = jnp.zeros((NODES2, 128), jnp.int32)
    for n in range(NODES2):
        at = (n % 2) * 8 + n // 2
        owner = jnp.where(line == at, feat2[n], owner)
        cut = jnp.where(line == at, bin2[n], cut)
    local = owner - feat * features
    select = jnp.where(local == iota((NODES2, 128), 1), 1.0, 0.0).astype(bf16)[:, 0:features]
    packed[0] = grad[...].astype(f32)
    packed[1] = hess[...].astype(f32)
    packed[2] = node_in[...].astype(f32)
    packed[3] = margin[...]
    values = bins[...].astype(f32)
    picked = lax.dot_general(select, values.astype(bf16), (((1,), (0,)), ((), ())), preferred_element_type=f32)
    picked_s[...] = jnp.where(picked > cut[:, 0:1].astype(f32), 1.0, 0.0)
    node = row(2)
    lo = jnp.where(values >= 2.0 * SEG, 2.0, jnp.where(values >= 1.0 * SEG, 1.0, 0.0))
    lo_s[...] = lo
    hi_s[...] = values - SEG * lo
    h = iota((2 * FOLD, B), 0)
    for k in range(LO):
        tri[k] = jnp.where((h + k * SEG <= iota((2 * FOLD, B), 1)) & (h < SEG), 1.0, 0.0).astype(bf16)
    for copy in route1:
        copy.wait_recv()
    right = x1[0] + x1[1] + x1[2] + x1[3]
    child = jnp.where(right > 0.5, 8.0, 0.0) + node
    member = child == iota((NODES2, count), 0).astype(f32)
    dir_s[1] = child
    w_s[0:16, :] = jnp.where(member, row(0), 0.0).astype(bf16)
    w_s[16:32, :] = jnp.where(member, row(1), 0.0).astype(bf16)
    x2[3] = jnp.max(jnp.where(member, picked_s[...], 0.0), axis=0, keepdims=True)
    route2 = [remote(x2.at[3], x2.at[d - 1], x2_ss.at[d - 1], x2_rs.at[d - 1], across(d)) for d in (1, 2, 3)]
    for copy in route2:
        copy.start()

    def feature(i, j, q):
        zo = (z + 1 + i * (1 - q) + j * q) % 4
        yo = (y + 1 + j * (1 - q) + i * q) % 4
        return zo * 16 + yo * 4 + q * 2

    hi_slots = iota((HI, count), 0).astype(f32).astype(bf16)

    def histogram(f):
        table_hi = jnp.where(hi_s[pl.ds(f, 1), :].astype(bf16) == hi_slots, bf16(1), bf16(0))
        lo_row = jnp.broadcast_to(lo_s[pl.ds(f, 1), :].astype(bf16), (COLS, count))
        weights = w_s[...]
        terms = jnp.concatenate([jnp.where(lo_row == bf16(k), weights, bf16(0)) for k in range(LO)], 0)
        return lax.dot_general(table_hi, terms, NT, preferred_element_type=f32)

    def core_copy(t):
        return remote(sent.at[t], mate.at[t], core_ss.at[t], core_rs.at[t], sibling)

    def p1_copy(t, slot, j):
        return remote(kept.at[t], part1.at[slot], p1_ss.at[slot], p1_rs.at[slot], inner(j + 1))

    def cross_copy():
        return remote(sent.at[14], part1.at[12], p1_ss.at[12], p1_rs.at[12], cross(1, 1 - c))

    def p2_copy(i):
        return remote(kept.at[OWN[i]], part2.at[i], p2_ss.at[i], p2_rs.at[i], outer(i + 1))

    def finish(t):
        core_copy(t).wait_recv()
        kept[t] += mate[t]

    def gather_plane(i):
        for j in range(3):
            p1_copy(0, i * 3 + j, j).wait_recv()
        kept[OWN[i]] += part1[i * 3] + part1[i * 3 + 1] + part1[i * 3 + 2]
        p2_copy(i).start()

    def leaf_copy(k):
        if k == 0:
            return [remote(sums.at[0], leaf_mate, leaf_ss.at[0], leaf_rs.at[0], sibling)]
        axis, dst = (inner, leaf_in) if k == 1 else (outer, leaf_out)
        return [remote(sums.at[k], dst.at[d - 1], leaf_ss.at[3 * k - 3 + d], leaf_rs.at[3 * k - 3 + d], axis(d)) for d in (1, 2, 3)]

    def leaves_0():
        for copy in route2:
            copy.wait_recv()
        right2 = jnp.where(x2[0] + x2[1] + x2[2] + x2[3] > 0.5, 1.0, 0.0)
        dir_s[0] = right2
        slot = iota((8, count), 0)
        sides = jnp.where(slot == 0, right2, jnp.where(slot == 1, 1.0 - right2, 0.0)).astype(bf16)
        sums[...] = jnp.zeros_like(sums)
        sums[0, :, 0:8] = lax.dot_general(w_s[...], sides, NT, preferred_element_type=f32)
        leaf_copy(0)[0].start()

    def leaves_1():
        leaf_copy(0)[0].wait_recv()
        sums[1] = sums[0] + leaf_mate[...]
        for copy in leaf_copy(1):
            copy.start()

    def leaves_2():
        for copy in leaf_copy(1):
            copy.wait_recv()
        sums[2] = sums[1] + leaf_in[0] + leaf_in[1] + leaf_in[2]
        for copy in leaf_copy(2):
            copy.start()

    def leaves_3():
        for copy in leaf_copy(2):
            copy.wait_recv()
        total = sums[2] + leaf_out[0] + leaf_out[1] + leaf_out[2]
        weight = -RATE * total[0:16] / (total[16:32] + LAMBDA)
        went = dir_s[0] > 0.5
        mine = dir_s[1] == iota((NODES2, count), 0).astype(f32)
        pick = jnp.where(went, weight[:, 0:1], weight[:, 1:2])
        result = row(3) + jnp.sum(jnp.where(mine, pick, 0.0), axis=0, keepdims=True)
        for r in range(lines):
            out_margin[r:r + 1, :] = result[:, r * 128:(r + 1) * 128]
        stores[2].start()

    def place(t):
        own, v = t // 9, t % 9
        late = v // 4
        mid = (v // 2) * (1 - late)
        at2, at3 = mid * (1 - v % 2), mid * (v % 2)
        i = (1 - own) * (v // 3) + own * (v + at2 - at3 - late)
        j = (1 - own) * (v % 3) + own * (3 - 2 * at2 - late)
        return i, j

    def fill(dst, t, f, slot):
        for e in range(2):
            wide[slot, e, :, 0:LO * COLS] = histogram(f + e)
        one, two = wide[slot, 0], wide[slot, 1]
        lane = iota((HI, 128), 1)
        dst[t, 0:HI] = jnp.where(lane < LO * COLS, one, pltpu.roll(two, COLS, 1))
        below = jnp.concatenate([two[FOLD:HI], jnp.zeros((2 * FOLD - HI, 128), f32)], 0)
        dst[t, HI:HI + FOLD] = jnp.where(lane[0:FOLD] < 64, two[0:FOLD], pltpu.roll(below, 64, 1))

    def compute_sent(t, i, j, slot):
        fill(sent, t, feature(i, j, 1 - c), 2 * slot)

    def compute_kept(t, i, j, slot):
        fill(kept, t, feature(i, j, c), 2 * slot + 1)

    def step(turn, carry):
        for s in range(2):
            t = turn * 2 + s
            compute_sent(t, *place(t), s)
            compute_kept(t, *place(t), s)
        for s in range(2):
            core_copy(turn * 2 + s).start()

        @pl.when((turn > 0) & (turn < 5))
        def _():
            for s in range(2):
                t = turn * 2 - 2 + s
                finish(t)
                p1_copy(t, t, t % 3).start()

        @pl.when(turn == 5)
        def _():
            finish(8)
            p1_copy(8, 8, 2).start()
            finish(9)
            gather_plane(0)

        @pl.when(turn == 6)
        def _():
            finish(11)
            p1_copy(11, 9, 1).start()
            finish(10)
            gather_plane(1)

        for k, action in enumerate((leaves_0, leaves_1, leaves_2)):
            pl.when(turn == (1, 2, 4)[k])(action)
        return carry

    lax.fori_loop(0, 7, step, 0)
    compute_sent(14, 3, 0, 0)
    cross_copy().start()
    compute_kept(14, 3, 0, 0)
    p1_copy(14, 11, 0).start()
    finish(13)
    p1_copy(13, 10, 2).start()
    finish(12)
    gather_plane(2)
    compute_sent(15, 3, 3, 1)
    core_copy(15).start()
    compute_kept(15, 3, 3, 1)
    leaves_3()
    finish(15)
    for i in range(3):
        p2_copy(i).wait_recv()
    for t, slot, j in ((11, 9, 1), (13, 10, 2), (14, 11, 0)):
        p1_copy(t, slot, j).wait_recv()
    cross_copy().wait_recv()

    hist = (kept[15] + part2[0] + part2[1] + part2[2] + part1[9] + part1[10] + part1[11] + part1[12])

    def split(x):
        a = x.astype(bf16)
        rest = x - a.astype(f32)
        b = rest.astype(bf16)
        return (rest - b.astype(f32)).astype(bf16), b, a

    def summed(pieces, ones):
        return sum(lax.dot_general(piece, ones, TN, preferred_element_type=f32) for piece in pieces)

    upper = split(jnp.concatenate([hist[0:HI], jnp.zeros((2 * FOLD - HI, 128), f32)], 0))
    folded = split(hist[HI:HI + FOLD])
    tops = [summed(upper, tri[k]) for k in range(LO)]
    first_half = [summed(folded, tri[k, 0:FOLD]) for k in range(2)]
    second_half = [summed(folded, tri[k, FOLD:2 * FOLD]) for k in range(2)]
    totals = (tops[0][0:32] + tops[1][32:64] + tops[2][64:96],
              first_half[0][0:32] + second_half[0][64:96] + first_half[1][32:64] + second_half[1][96:128] + tops[2][96:128])
    for e, total in enumerate(totals):
        g2, h2 = total[0:16], total[16:32]
        for grad_left, hess_left, out, stride in (
            (g2[0:8] + g2[8:16], h2[0:8] + h2[8:16], out1, 1), (g2, h2, out2, 2)):
            grad_total = grad_left[:, B - 1:B]
            hess_total = hess_left[:, B - 1:B]
            grad_right = grad_total - grad_left
            hess_right = hess_total - hess_left
            gain = (grad_left * grad_left / (hess_left + LAMBDA)
                    + grad_right * grad_right / (hess_right + LAMBDA)
                    - grad_total * grad_total / (hess_total + LAMBDA))
            for side in range(stride):
                for n in range(NODES1):
                    out[n * stride + side, e:e + 1, :] = gain[side * 8 + n:side * 8 + n + 1]

    for copy in stores[:2]:
        copy.start()
    for copy in route1 + route2 + leaf_copy(0) + leaf_copy(1) + leaf_copy(2):
        copy.wait_send()
    for t in list(range(14)) + [15]:
        core_copy(t).wait_send()
    for t in range(9):
        p1_copy(t, t, t % 3).wait_send()
    for t, slot, j in ((11, 9, 1), (13, 10, 2), (14, 11, 0)):
        p1_copy(t, slot, j).wait_send()
    cross_copy().wait_send()
    for i in range(3):
        p2_copy(i).wait_send()
    for copy in stores:
        copy.wait()


def copy_kernel(a, b, d, a_out, b_out, d_out):
    for src, dst in ((a, a_out), (b, b_out), (d, d_out)):
        dst[...] = src[...]


def hand_out(*arrays):
    return pl.pallas_call(
        copy_kernel,
        out_shape=tuple(jax.ShapeDtypeStruct(a.shape, a.dtype) for a in arrays),
        in_specs=[pl.BlockSpec(memory_space=pltpu.VMEM)] * 3,
        out_specs=[pl.BlockSpec(memory_space=pltpu.VMEM)] * 3,
        name="hand_out",
    )(*arrays)


def body(bins, grad, hess, margin, node_start, split_feat1, split_bin1, split_feat2, split_bin2):
    features, count = bins.shape
    lines = (count // 128, 128)
    own = features * 4 // 128
    dma = pltpu.SemaphoreType.DMA
    pair = (HI + FOLD, 128)
    gain1, gain2, new_margin = pl.pallas_call(
        kernel,
        out_shape=(
            jax.ShapeDtypeStruct((NODES1, own, B), f32),
            jax.ShapeDtypeStruct((NODES2, own, B), f32),
            jax.ShapeDtypeStruct(lines, f32)),
        in_specs=[pl.BlockSpec(memory_space=pltpu.HBM)] * 9,
        out_specs=[pl.BlockSpec(memory_space=pltpu.HBM)] * 3,
        scratch_shapes=[
            pltpu.VMEM((features, count), jnp.int32),
            pltpu.VMEM(lines, bf16),
            pltpu.VMEM(lines, bf16),
            pltpu.VMEM(lines, f32),
            pltpu.VMEM(lines, jnp.int32),
            pltpu.SMEM((NODES1,), jnp.int32),
            pltpu.SMEM((NODES1,), jnp.int32),
            pltpu.SMEM((NODES2,), jnp.int32),
            pltpu.SMEM((NODES2,), jnp.int32),
            pltpu.VMEM((NODES1, own, B), f32),
            pltpu.VMEM((NODES2, own, B), f32),
            pltpu.VMEM(lines, f32),
            pltpu.VMEM((4,) + lines, f32),
            pltpu.VMEM((NODES1, count), jnp.int32),
            dma((9,)), dma((3,)),
            pltpu.VMEM((features, count), f32),
            pltpu.VMEM((features, count), f32),
            pltpu.VMEM((COLS, count), bf16),
            pltpu.VMEM((NODES2, count), f32),
            pltpu.VMEM((2, 1, count), f32),
            pltpu.VMEM((16,) + pair, f32),
            pltpu.VMEM((16,) + pair, f32),
            pltpu.VMEM((16,) + pair, f32),
            pltpu.VMEM((13,) + pair, f32),
            pltpu.VMEM((3,) + pair, f32),
            pltpu.VMEM((3, COLS, 128), f32),
            pltpu.VMEM((LO, 2 * FOLD, B), bf16),
            pltpu.VMEM((4, 1, count), f32),
            pltpu.VMEM((4, 1, count), f32),
            pltpu.VMEM((COLS, 128), f32),
            pltpu.VMEM((3, COLS, 128), f32),
            pltpu.VMEM((3, COLS, 128), f32),
            pltpu.VMEM((4, 2, HI, 128), f32),
            dma((3,)), dma((3,)), dma((3,)), dma((3,)),
            dma((16,)), dma((16,)), dma((13,)), dma((13,)), dma((3,)), dma((3,)),
            dma((7,)), dma((7,)),
        ],
        compiler_params=pltpu.CompilerParams(
            collective_id=0, has_side_effects=True, vmem_limit_bytes=60 * 2**20),
        cost_estimate=pl.CostEstimate(flops=2 * 64 * 4096 * 8192, bytes_accessed=2**20, transcendentals=0),
    )(bins, grad.reshape(lines), hess.reshape(lines), margin.reshape(lines), node_start.reshape(lines),
      split_feat1, split_bin1, split_feat2, split_bin2)
    gain1, gain2, new_margin = hand_out(gain1, gain2, new_margin)
    return gain1, gain2, new_margin.reshape(count)


def solution(mesh):
    return jax.shard_map(
        body,
        mesh=mesh,
        in_specs=(P("feat", "row"), P("row"), P("row"), P("row"), P("row"), P(), P(), P(), P()),
        out_specs=(P(None, ("feat", "row"), None), P(None, ("feat", "row"), None), P("row")),
        check_vma=False,
    )
```

```python
import jax
import jax.numpy as jnp
from jax import lax
from jax.experimental import pallas as pl
from jax.experimental.pallas import tpu as pltpu
from jax.sharding import PartitionSpec as P

B = 256
NODES1 = 8
NODES2 = 16
LAMBDA = 1.0
RATE = 0.3

SEG = 86
HI = 88
FOLD = 48
LO = 3
COLS = 2 * NODES2
OWN = (9, 10, 12)

MESH = pl.DeviceIdType.MESH
NT = (((1,), (1,)), ((), ()))
TN = (((0,), (0,)), ((), ()))
f32 = jnp.float32
bf16 = jnp.bfloat16


def iota(shape, dim):
    return lax.broadcasted_iota(jnp.int32, shape, dim)


def kernel(bins_hbm, grad_hbm, hess_hbm, margin_hbm, node_hbm, feat1_hbm, bin1_hbm, feat2_hbm, bin2_hbm,
           out1_hbm, out2_hbm, margin_out_hbm,
           bins, grad, hess, margin, node_in, feat1, bin1, feat2, bin2, out1, out2, out_margin,
           packed, first_s, in_sem, out_sem, hi_s, lo_s, w_s, picked_s, dir_s, kept, sent, mate, part1, part2, sums, tri,
           x1, x2, leaf_mate, leaf_in, leaf_out, wide,
           x1_ss, x1_rs, x2_ss, x2_rs, core_ss, core_rs, p1_ss, p1_rs, p2_ss, p2_rs, leaf_ss, leaf_rs):
    features, count = bins.shape
    lines = count // 128
    loads = [pltpu.make_async_copy(src, dst, in_sem.at[k]) for k, (src, dst) in enumerate((
        (bins_hbm, bins), (node_hbm, node_in), (feat1_hbm, feat1), (bin1_hbm, bin1), (feat2_hbm, feat2), (bin2_hbm, bin2),
        (grad_hbm, grad), (hess_hbm, hess), (margin_hbm, margin)))]
    stores = [pltpu.make_async_copy(src, dst, out_sem.at[k]) for k, (src, dst) in enumerate((
        (out1, out1_hbm), (out2, out2_hbm), (out_margin, margin_out_hbm)))]
    for copy in loads:
        copy.start()

    def row(k):
        return jnp.concatenate([packed[k, r:r + 1, :] for r in range(lines)], axis=1)

    me = lax.axis_index("row")
    feat = lax.axis_index("feat")
    z, y, c = me // 8, (me // 2) % 4, me % 2

    def inner(d):
        return (((z + d * c) % 4) * 8 + ((y + d * (1 - c)) % 4) * 2 + c, feat)

    def outer(d):
        return (((z + d * (1 - c)) % 4) * 8 + ((y + d * c) % 4) * 2 + c, feat)

    def cross(d, q):
        return (((z + d * q) % 4) * 8 + ((y + d * (1 - q)) % 4) * 2 + q, feat)

    sibling = (z * 8 + y * 2 + (1 - c), feat)

    def across(d):
        return (me, (feat + d) % 4)

    peers = [sibling] + [axis(d) for axis in (inner, outer, across) for d in (1, 2, 3)]
    peers.append((((z + 3 * c) % 4) * 8 + ((y + 3 - 3 * c) % 4) * 2 + 1 - c, feat))
    barrier = pltpu.get_barrier_semaphore()
    for peer in peers:
        pl.semaphore_signal(barrier, inc=1, device_id=peer, device_id_type=MESH)

    def remote(src, dst, ss, rs, peer):
        return pltpu.make_async_remote_copy(
            src_ref=src, dst_ref=dst, send_sem=ss, recv_sem=rs, device_id=peer, device_id_type=MESH)

    for copy in loads[:4]:
        copy.wait()
    slot8 = iota((NODES1, 128), 0)
    low = jnp.full((NODES1, 128), B, jnp.int32)
    for n in range(NODES1):
        at = feat1[n] - feat * features
        inside = jnp.clip(at, 0, features - 1)
        first_s[n:n + 1, :] = bins[pl.ds(inside, 1), :]
        low = jnp.where((slot8 == n) & (jnp.full((NODES1, 128), at, jnp.int32) == inside), bin1[n], low)
    node_rows = jnp.concatenate([node_in[r:r + 1, :] for r in range(lines)], axis=1)
    taken = (first_s[...] > low[:, 0:1]) & (node_rows == iota((NODES1, count), 0))
    x1[3] = jnp.max(jnp.where(taken, 1.0, 0.0), axis=0, keepdims=True)
    pl.semaphore_wait(barrier, len(peers))
    route1 = [remote(x1.at[3], x1.at[d - 1], x1_ss.at[d - 1], x1_rs.at[d - 1], across(d)) for d in (1, 2, 3)]
    for copy in route1:
        copy.start()

    for copy in loads[4:]:
        copy.wait()
    line = iota((NODES2, 128), 0)
    owner = jnp.full((NODES2, 128), -1, jnp.int32)
    cut = jnp.zeros((NODES2, 128), jnp.int32)
    for n in range(NODES2):
        at = (n % 2) * 8 + n // 2
        owner = jnp.where(line == at, feat2[n], owner)
        cut = jnp.where(line == at, bin2[n], cut)
    local = owner - feat * features
    select = jnp.where(local == iota((NODES2, 128), 1), 1.0, 0.0).astype(bf16)[:, 0:features]
    packed[0] = grad[...].astype(f32)
    packed[1] = hess[...].astype(f32)
    packed[2] = node_in[...].astype(f32)
    packed[3] = margin[...]
    values = bins[...].astype(f32)
    picked = lax.dot_general(select, values.astype(bf16), (((1,), (0,)), ((), ())), preferred_element_type=f32)
    picked_s[...] = jnp.where(picked > cut[:, 0:1].astype(f32), 1.0, 0.0)
    node = row(2)
    lo = jnp.where(values >= 2.0 * SEG, 2.0, jnp.where(values >= 1.0 * SEG, 1.0, 0.0))
    lo_s[...] = lo
    hi_s[...] = values - SEG * lo
    h = iota((2 * FOLD, B), 0)
    for k in range(LO):
        tri[k] = jnp.where((h + k * SEG <= iota((2 * FOLD, B), 1)) & (h < SEG), 1.0, 0.0).astype(bf16)
    for copy in route1:
        copy.wait_recv()
    right = x1[0] + x1[1] + x1[2] + x1[3]
    child = jnp.where(right > 0.5, 8.0, 0.0) + node
    member = child == iota((NODES2, count), 0).astype(f32)
    dir_s[1] = child
    w_s[0:16, :] = jnp.where(member, row(0), 0.0).astype(bf16)
    w_s[16:32, :] = jnp.where(member, row(1), 0.0).astype(bf16)
    x2[3] = jnp.max(jnp.where(member, picked_s[...], 0.0), axis=0, keepdims=True)
    route2 = [remote(x2.at[3], x2.at[d - 1], x2_ss.at[d - 1], x2_rs.at[d - 1], across(d)) for d in (1, 2, 3)]
    for copy in route2:
        copy.start()

    def feature(i, j, q):
        zo = (z + 1 + i * (1 - q) + j * q) % 4
        yo = (y + 1 + j * (1 - q) + i * q) % 4
        return zo * 16 + yo * 4 + q * 2

    hi_slots = iota((HI, count), 0).astype(f32).astype(bf16)

    def histogram(f):
        table_hi = jnp.where(hi_s[pl.ds(f, 1), :].astype(bf16) == hi_slots, bf16(1), bf16(0))
        lo_row = jnp.broadcast_to(lo_s[pl.ds(f, 1), :].astype(bf16), (COLS, count))
        weights = w_s[...]
        terms = jnp.concatenate([jnp.where(lo_row == bf16(k), weights, bf16(0)) for k in range(LO)], 0)
        return lax.dot_general(table_hi, terms, NT, preferred_element_type=f32)

    def core_copy(t):
        return remote(sent.at[t], mate.at[t], core_ss.at[t], core_rs.at[t], sibling)

    def p1_copy(t, slot, j):
        return remote(kept.at[t], part1.at[slot], p1_ss.at[slot], p1_rs.at[slot], inner(j + 1))

    def cross_copy():
        return remote(sent.at[14], part1.at[12], p1_ss.at[12], p1_rs.at[12], cross(1, 1 - c))

    def p2_copy(i):
        return remote(kept.at[OWN[i]], part2.at[i], p2_ss.at[i], p2_rs.at[i], outer(i + 1))

    def finish(t):
        core_copy(t).wait_recv()
        kept[t] += mate[t]

    def gather_plane(i):
        for j in range(3):
            p1_copy(0, i * 3 + j, j).wait_recv()
        kept[OWN[i]] += part1[i * 3] + part1[i * 3 + 1] + part1[i * 3 + 2]
        p2_copy(i).start()

    def leaf_copy(k):
        if k == 0:
            return [remote(sums.at[0], leaf_mate, leaf_ss.at[0], leaf_rs.at[0], sibling)]
        axis, dst = (inner, leaf_in) if k == 1 else (outer, leaf_out)
        return [remote(sums.at[k], dst.at[d - 1], leaf_ss.at[3 * k - 3 + d], leaf_rs.at[3 * k - 3 + d], axis(d)) for d in (1, 2, 3)]

    def leaves_0():
        for copy in route2:
            copy.wait_recv()
        right2 = jnp.where(x2[0] + x2[1] + x2[2] + x2[3] > 0.5, 1.0, 0.0)
        dir_s[0] = right2
        slot = iota((8, count), 0)
        sides = jnp.where(slot == 0, right2, jnp.where(slot == 1, 1.0 - right2, 0.0)).astype(bf16)
        sums[...] = jnp.zeros_like(sums)
        sums[0, :, 0:8] = lax.dot_general(w_s[...], sides, NT, preferred_element_type=f32)
        leaf_copy(0)[0].start()

    def leaves_1():
        leaf_copy(0)[0].wait_recv()
        sums[1] = sums[0] + leaf_mate[...]
        for copy in leaf_copy(1):
            copy.start()

    def leaves_2():
        for copy in leaf_copy(1):
            copy.wait_recv()
        sums[2] = sums[1] + leaf_in[0] + leaf_in[1] + leaf_in[2]
        for copy in leaf_copy(2):
            copy.start()

    def leaves_3():
        for copy in leaf_copy(2):
            copy.wait_recv()
        total = sums[2] + leaf_out[0] + leaf_out[1] + leaf_out[2]
        weight = -RATE * total[0:16] / (total[16:32] + LAMBDA)
        went = dir_s[0] > 0.5
        mine = dir_s[1] == iota((NODES2, count), 0).astype(f32)
        pick = jnp.where(went, weight[:, 0:1], weight[:, 1:2])
        result = row(3) + jnp.sum(jnp.where(mine, pick, 0.0), axis=0, keepdims=True)
        for r in range(lines):
            out_margin[r:r + 1, :] = result[:, r * 128:(r + 1) * 128]
        stores[2].start()

    def place(t):
        own, v = t // 9, t % 9
        late = v // 4
        mid = (v // 2) * (1 - late)
        at2, at3 = mid * (1 - v % 2), mid * (v % 2)
        i = (1 - own) * (v // 3) + own * (v + at2 - at3 - late)
        j = (1 - own) * (v % 3) + own * (3 - 2 * at2 - late)
        return i, j

    def fill(dst, t, f, slot):
        for e in range(2):
            wide[slot, e, :, 0:LO * COLS] = histogram(f + e)
        one, two = wide[slot, 0], wide[slot, 1]
        lane = iota((HI, 128), 1)
        dst[t, 0:HI] = jnp.where(lane < LO * COLS, one, pltpu.roll(two, COLS, 1))
        below = jnp.concatenate([two[FOLD:HI], jnp.zeros((2 * FOLD - HI, 128), f32)], 0)
        dst[t, HI:HI + FOLD] = jnp.where(lane[0:FOLD] < 64, two[0:FOLD], pltpu.roll(below, 64, 1))

    def compute_sent(t, i, j, slot):
        fill(sent, t, feature(i, j, 1 - c), 2 * slot)

    def compute_kept(t, i, j, slot):
        fill(kept, t, feature(i, j, c), 2 * slot + 1)

    def step(turn, carry):
        for s in range(2):
            t = turn * 2 + s
            compute_sent(t, *place(t), s)
            compute_kept(t, *place(t), s)
        for s in range(2):
            core_copy(turn * 2 + s).start()

        @pl.when((turn > 0) & (turn < 5))
        def _():
            for s in range(2):
                t = turn * 2 - 2 + s
                finish(t)
                p1_copy(t, t, t % 3).start()

        @pl.when(turn == 5)
        def _():
            finish(8)
            p1_copy(8, 8, 2).start()
            finish(9)
            gather_plane(0)

        @pl.when(turn == 6)
        def _():
            finish(11)
            p1_copy(11, 9, 1).start()
            finish(10)
            gather_plane(1)

        for k, action in enumerate((leaves_0, leaves_1, leaves_2)):
            pl.when(turn == (1, 2, 4)[k])(action)
        return carry

    lax.fori_loop(0, 7, step, 0)
    compute_sent(14, 3, 0, 0)
    cross_copy().start()
    compute_kept(14, 3, 0, 0)
    p1_copy(14, 11, 0).start()
    compute_sent(15, 3, 3, 1)
    core_copy(15).start()
    finish(13)
    p1_copy(13, 10, 2).start()
    finish(12)
    gather_plane(2)
    compute_kept(15, 3, 3, 1)
    leaves_3()
    finish(15)
    for i in range(3):
        p2_copy(i).wait_recv()
    for t, slot, j in ((11, 9, 1), (13, 10, 2), (14, 11, 0)):
        p1_copy(t, slot, j).wait_recv()
    cross_copy().wait_recv()

    hist = (kept[15] + part2[0] + part2[1] + part2[2] + part1[9] + part1[10] + part1[11] + part1[12])

    def split(x):
        a = x.astype(bf16)
        rest = x - a.astype(f32)
        b = rest.astype(bf16)
        return (rest - b.astype(f32)).astype(bf16), b, a

    def summed(pieces, ones):
        return sum(lax.dot_general(piece, ones, TN, preferred_element_type=f32) for piece in pieces)

    upper = split(jnp.concatenate([hist[0:HI], jnp.zeros((2 * FOLD - HI, 128), f32)], 0))
    folded = split(hist[HI:HI + FOLD])
    tops = [summed(upper, tri[k]) for k in range(LO)]
    first_half = [summed(folded, tri[k, 0:FOLD]) for k in range(2)]
    second_half = [summed(folded, tri[k, FOLD:2 * FOLD]) for k in range(2)]
    totals = (tops[0][0:32] + tops[1][32:64] + tops[2][64:96],
              first_half[0][0:32] + second_half[0][64:96] + first_half[1][32:64] + second_half[1][96:128] + tops[2][96:128])
    for e, total in enumerate(totals):
        g2, h2 = total[0:16], total[16:32]
        for grad_left, hess_left, out, stride in (
            (g2[0:8] + g2[8:16], h2[0:8] + h2[8:16], out1, 1), (g2, h2, out2, 2)):
            grad_total = grad_left[:, B - 1:B]
            hess_total = hess_left[:, B - 1:B]
            grad_right = grad_total - grad_left
            hess_right = hess_total - hess_left
            gain = (grad_left * grad_left / (hess_left + LAMBDA)
                    + grad_right * grad_right / (hess_right + LAMBDA)
                    - grad_total * grad_total / (hess_total + LAMBDA))
            for side in range(stride):
                for n in range(NODES1):
                    out[n * stride + side, e:e + 1, :] = gain[side * 8 + n:side * 8 + n + 1]

    for copy in stores[:2]:
        copy.start()
    for copy in route1 + route2 + leaf_copy(0) + leaf_copy(1) + leaf_copy(2):
        copy.wait_send()
    for t in list(range(14)) + [15]:
        core_copy(t).wait_send()
    for t in range(9):
        p1_copy(t, t, t % 3).wait_send()
    for t, slot, j in ((11, 9, 1), (13, 10, 2), (14, 11, 0)):
        p1_copy(t, slot, j).wait_send()
    cross_copy().wait_send()
    for i in range(3):
        p2_copy(i).wait_send()
    for copy in stores:
        copy.wait()


def copy_kernel(a, b, d, a_out, b_out, d_out):
    for src, dst in ((a, a_out), (b, b_out), (d, d_out)):
        dst[...] = src[...]


def hand_out(*arrays):
    return pl.pallas_call(
        copy_kernel,
        out_shape=tuple(jax.ShapeDtypeStruct(a.shape, a.dtype) for a in arrays),
        in_specs=[pl.BlockSpec(memory_space=pltpu.VMEM)] * 3,
        out_specs=[pl.BlockSpec(memory_space=pltpu.VMEM)] * 3,
        name="hand_out",
    )(*arrays)


def body(bins, grad, hess, margin, node_start, split_feat1, split_bin1, split_feat2, split_bin2):
    features, count = bins.shape
    lines = (count // 128, 128)
    own = features * 4 // 128
    dma = pltpu.SemaphoreType.DMA
    pair = (HI + FOLD, 128)
    gain1, gain2, new_margin = pl.pallas_call(
        kernel,
        out_shape=(
            jax.ShapeDtypeStruct((NODES1, own, B), f32),
            jax.ShapeDtypeStruct((NODES2, own, B), f32),
            jax.ShapeDtypeStruct(lines, f32)),
        in_specs=[pl.BlockSpec(memory_space=pltpu.HBM)] * 9,
        out_specs=[pl.BlockSpec(memory_space=pltpu.HBM)] * 3,
        scratch_shapes=[
            pltpu.VMEM((features, count), jnp.int32),
            pltpu.VMEM(lines, bf16),
            pltpu.VMEM(lines, bf16),
            pltpu.VMEM(lines, f32),
            pltpu.VMEM(lines, jnp.int32),
            pltpu.SMEM((NODES1,), jnp.int32),
            pltpu.SMEM((NODES1,), jnp.int32),
            pltpu.SMEM((NODES2,), jnp.int32),
            pltpu.SMEM((NODES2,), jnp.int32),
            pltpu.VMEM((NODES1, own, B), f32),
            pltpu.VMEM((NODES2, own, B), f32),
            pltpu.VMEM(lines, f32),
            pltpu.VMEM((4,) + lines, f32),
            pltpu.VMEM((NODES1, count), jnp.int32),
            dma((9,)), dma((3,)),
            pltpu.VMEM((features, count), f32),
            pltpu.VMEM((features, count), f32),
            pltpu.VMEM((COLS, count), bf16),
            pltpu.VMEM((NODES2, count), f32),
            pltpu.VMEM((2, 1, count), f32),
            pltpu.VMEM((16,) + pair, f32),
            pltpu.VMEM((16,) + pair, f32),
            pltpu.VMEM((16,) + pair, f32),
            pltpu.VMEM((13,) + pair, f32),
            pltpu.VMEM((3,) + pair, f32),
            pltpu.VMEM((3, COLS, 128), f32),
            pltpu.VMEM((LO, 2 * FOLD, B), bf16),
            pltpu.VMEM((4, 1, count), f32),
            pltpu.VMEM((4, 1, count), f32),
            pltpu.VMEM((COLS, 128), f32),
            pltpu.VMEM((3, COLS, 128), f32),
            pltpu.VMEM((3, COLS, 128), f32),
            pltpu.VMEM((4, 2, HI, 128), f32),
            dma((3,)), dma((3,)), dma((3,)), dma((3,)),
            dma((16,)), dma((16,)), dma((13,)), dma((13,)), dma((3,)), dma((3,)),
            dma((7,)), dma((7,)),
        ],
        compiler_params=pltpu.CompilerParams(
            collective_id=0, has_side_effects=True, vmem_limit_bytes=60 * 2**20),
        cost_estimate=pl.CostEstimate(flops=2 * 64 * 4096 * 8192, bytes_accessed=2**20, transcendentals=0),
    )(bins, grad.reshape(lines), hess.reshape(lines), margin.reshape(lines), node_start.reshape(lines),
      split_feat1, split_bin1, split_feat2, split_bin2)
    gain1, gain2, new_margin = hand_out(gain1, gain2, new_margin)
    return gain1, gain2, new_margin.reshape(count)


def solution(mesh):
    return jax.shard_map(
        body,
        mesh=mesh,
        in_specs=(P("feat", "row"), P("row"), P("row"), P("row"), P("row"), P(), P(), P(), P()),
        out_specs=(P(None, ("feat", "row"), None), P(None, ("feat", "row"), None), P("row")),
        check_vma=False,
    )
```

```python
import jax
import jax.numpy as jnp
from jax import lax
from jax.experimental import pallas as pl
from jax.experimental.pallas import tpu as pltpu
from jax.sharding import PartitionSpec as P

B = 256
NODES1 = 8
NODES2 = 16
LAMBDA = 1.0
RATE = 0.3

SEG = 86
HI = 88
FOLD = 48
LO = 3
COLS = 2 * NODES2
OWN = (9, 10, 12)

MESH = pl.DeviceIdType.MESH
NT = (((1,), (1,)), ((), ()))
TN = (((0,), (0,)), ((), ()))
f32 = jnp.float32
bf16 = jnp.bfloat16


def iota(shape, dim):
    return lax.broadcasted_iota(jnp.int32, shape, dim)


def kernel(bins_hbm, grad_hbm, hess_hbm, margin_hbm, node_hbm, feat1_hbm, bin1_hbm, feat2_hbm, bin2_hbm,
           out1_hbm, out2_hbm, margin_out_hbm,
           bins, grad, hess, margin, node_in, feat1, bin1, feat2, bin2, out1, out2, out_margin,
           packed, first_s, in_sem, out_sem, hi_s, lo_s, w_s, picked_s, dir_s, kept, sent, mate, part1, part2, sums, tri,
           x1, x2, leaf_mate, leaf_in, leaf_out, wide,
           x1_ss, x1_rs, x2_ss, x2_rs, core_ss, core_rs, p1_ss, p1_rs, p2_ss, p2_rs, leaf_ss, leaf_rs):
    features, count = bins.shape
    lines = count // 128
    loads = [pltpu.make_async_copy(src, dst, in_sem.at[k]) for k, (src, dst) in enumerate((
        (bins_hbm, bins), (node_hbm, node_in), (feat1_hbm, feat1), (bin1_hbm, bin1), (feat2_hbm, feat2), (bin2_hbm, bin2),
        (grad_hbm, grad), (hess_hbm, hess), (margin_hbm, margin)))]
    stores = [pltpu.make_async_copy(src, dst, out_sem.at[k]) for k, (src, dst) in enumerate((
        (out1, out1_hbm), (out2, out2_hbm), (out_margin, margin_out_hbm)))]
    for copy in loads:
        copy.start()

    def row(k):
        return jnp.concatenate([packed[k, r:r + 1, :] for r in range(lines)], axis=1)

    me = lax.axis_index("row")
    feat = lax.axis_index("feat")
    z, y, c = me // 8, (me // 2) % 4, me % 2

    def inner(d):
        return (((z + d * c) % 4) * 8 + ((y + d * (1 - c)) % 4) * 2 + c, feat)

    def outer(d):
        return (((z + d * (1 - c)) % 4) * 8 + ((y + d * c) % 4) * 2 + c, feat)

    def cross(d, q):
        return (((z + d * q) % 4) * 8 + ((y + d * (1 - q)) % 4) * 2 + q, feat)

    sibling = (z * 8 + y * 2 + (1 - c), feat)

    def across(d):
        return (me, (feat + d) % 4)

    peers = [sibling] + [axis(d) for axis in (inner, outer, across) for d in (1, 2, 3)]
    peers.append((((z + 3 * c) % 4) * 8 + ((y + 3 - 3 * c) % 4) * 2 + 1 - c, feat))
    barrier = pltpu.get_barrier_semaphore()
    for peer in peers:
        pl.semaphore_signal(barrier, inc=1, device_id=peer, device_id_type=MESH)

    def remote(src, dst, ss, rs, peer):
        return pltpu.make_async_remote_copy(
            src_ref=src, dst_ref=dst, send_sem=ss, recv_sem=rs, device_id=peer, device_id_type=MESH)

    for copy in loads[:4]:
        copy.wait()
    slot8 = iota((NODES1, 128), 0)
    low = jnp.full((NODES1, 128), B, jnp.int32)
    for n in range(NODES1):
        at = feat1[n] - feat * features
        inside = jnp.clip(at, 0, features - 1)
        first_s[n:n + 1, :] = bins[pl.ds(inside, 1), :]
        low = jnp.where((slot8 == n) & (jnp.full((NODES1, 128), at, jnp.int32) == inside), bin1[n], low)
    node_rows = jnp.concatenate([node_in[r:r + 1, :] for r in range(lines)], axis=1)
    taken = (first_s[...] > low[:, 0:1]) & (node_rows == iota((NODES1, count), 0))
    x1[3] = jnp.max(jnp.where(taken, 1.0, 0.0), axis=0, keepdims=True)
    pl.semaphore_wait(barrier, len(peers))
    route1 = [remote(x1.at[3], x1.at[d - 1], x1_ss.at[d - 1], x1_rs.at[d - 1], across(d)) for d in (1, 2, 3)]
    for copy in route1:
        copy.start()

    for copy in loads[4:]:
        copy.wait()
    line = iota((NODES2, 128), 0)
    owner = jnp.full((NODES2, 128), -1, jnp.int32)
    cut = jnp.zeros((NODES2, 128), jnp.int32)
    for n in range(NODES2):
        at = (n % 2) * 8 + n // 2
        owner = jnp.where(line == at, feat2[n], owner)
        cut = jnp.where(line == at, bin2[n], cut)
    local = owner - feat * features
    select = jnp.where(local == iota((NODES2, 128), 1), 1.0, 0.0).astype(bf16)[:, 0:features]
    packed[0] = grad[...].astype(f32)
    packed[1] = hess[...].astype(f32)
    packed[2] = node_in[...].astype(f32)
    packed[3] = margin[...]
    values = bins[...].astype(f32)
    picked = lax.dot_general(select, values.astype(bf16), (((1,), (0,)), ((), ())), preferred_element_type=f32)
    picked_s[...] = jnp.where(picked > cut[:, 0:1].astype(f32), 1.0, 0.0)
    node = row(2)
    lo = jnp.where(values >= 2.0 * SEG, 2.0, jnp.where(values >= 1.0 * SEG, 1.0, 0.0))
    lo_s[...] = lo
    hi_s[...] = values - SEG * lo
    h = iota((2 * FOLD, B), 0)
    for k in range(LO):
        tri[k] = jnp.where((h + k * SEG <= iota((2 * FOLD, B), 1)) & (h < SEG), 1.0, 0.0).astype(bf16)
    for copy in route1:
        copy.wait_recv()
    right = x1[0] + x1[1] + x1[2] + x1[3]
    child = jnp.where(right > 0.5, 8.0, 0.0) + node
    member = child == iota((NODES2, count), 0).astype(f32)
    dir_s[1] = child
    w_s[0:16, :] = jnp.where(member, row(0), 0.0).astype(bf16)
    w_s[16:32, :] = jnp.where(member, row(1), 0.0).astype(bf16)
    x2[3] = jnp.max(jnp.where(member, picked_s[...], 0.0), axis=0, keepdims=True)
    route2 = [remote(x2.at[3], x2.at[d - 1], x2_ss.at[d - 1], x2_rs.at[d - 1], across(d)) for d in (1, 2, 3)]
    for copy in route2:
        copy.start()

    def feature(i, j, q):
        zo = (z + 1 + i * (1 - q) + j * q) % 4
        yo = (y + 1 + j * (1 - q) + i * q) % 4
        return zo * 16 + yo * 4 + q * 2

    hi_slots = iota((HI, count), 0).astype(f32).astype(bf16)

    def histogram(f):
        table_hi = jnp.where(hi_s[pl.ds(f, 1), :].astype(bf16) == hi_slots, bf16(1), bf16(0))
        lo_row = jnp.broadcast_to(lo_s[pl.ds(f, 1), :].astype(bf16), (COLS, count))
        weights = w_s[...]
        terms = jnp.concatenate([jnp.where(lo_row == bf16(k), weights, bf16(0)) for k in range(LO)], 0)
        return lax.dot_general(table_hi, terms, NT, preferred_element_type=f32)

    def core_copy(t):
        return remote(sent.at[t], mate.at[t], core_ss.at[t], core_rs.at[t], sibling)

    def p1_copy(t, slot, j):
        return remote(kept.at[t], part1.at[slot], p1_ss.at[slot], p1_rs.at[slot], inner(j + 1))

    def cross_copy():
        return remote(sent.at[14], part1.at[12], p1_ss.at[12], p1_rs.at[12], cross(1, 1 - c))

    def p2_copy(i):
        return remote(kept.at[OWN[i]], part2.at[i], p2_ss.at[i], p2_rs.at[i], outer(i + 1))

    def finish(t):
        core_copy(t).wait_recv()
        kept[t] += mate[t]

    def gather_plane(i):
        for j in range(3):
            p1_copy(0, i * 3 + j, j).wait_recv()
        kept[OWN[i]] += part1[i * 3] + part1[i * 3 + 1] + part1[i * 3 + 2]
        p2_copy(i).start()

    def leaf_copy(k):
        if k == 0:
            return [remote(sums.at[0], leaf_mate, leaf_ss.at[0], leaf_rs.at[0], sibling)]
        axis, dst = (inner, leaf_in) if k == 1 else (outer, leaf_out)
        return [remote(sums.at[k], dst.at[d - 1], leaf_ss.at[3 * k - 3 + d], leaf_rs.at[3 * k - 3 + d], axis(d)) for d in (1, 2, 3)]

    def leaves_0():
        for copy in route2:
            copy.wait_recv()
        right2 = jnp.where(x2[0] + x2[1] + x2[2] + x2[3] > 0.5, 1.0, 0.0)
        dir_s[0] = right2
        slot = iota((8, count), 0)
        sides = jnp.where(slot == 0, right2, jnp.where(slot == 1, 1.0 - right2, 0.0)).astype(bf16)
        sums[...] = jnp.zeros_like(sums)
        sums[0, :, 0:8] = lax.dot_general(w_s[...], sides, NT, preferred_element_type=f32)
        leaf_copy(0)[0].start()

    def leaves_1():
        leaf_copy(0)[0].wait_recv()
        sums[1] = sums[0] + leaf_mate[...]
        for copy in leaf_copy(1):
            copy.start()

    def leaves_2():
        for copy in leaf_copy(1):
            copy.wait_recv()
        sums[2] = sums[1] + leaf_in[0] + leaf_in[1] + leaf_in[2]
        for copy in leaf_copy(2):
            copy.start()

    def leaves_3():
        for copy in leaf_copy(2):
            copy.wait_recv()
        total = sums[2] + leaf_out[0] + leaf_out[1] + leaf_out[2]
        weight = -RATE * total[0:16] / (total[16:32] + LAMBDA)
        went = dir_s[0] > 0.5
        mine = dir_s[1] == iota((NODES2, count), 0).astype(f32)
        pick = jnp.where(went, weight[:, 0:1], weight[:, 1:2])
        result = row(3) + jnp.sum(jnp.where(mine, pick, 0.0), axis=0, keepdims=True)
        for r in range(lines):
            out_margin[r:r + 1, :] = result[:, r * 128:(r + 1) * 128]
        stores[2].start()

    def place(t):
        own, v = t // 9, t % 9
        late = v // 4
        mid = (v // 2) * (1 - late)
        at2, at3 = mid * (1 - v % 2), mid * (v % 2)
        i = (1 - own) * (v // 3) + own * (v + at2 - at3 - late)
        j = (1 - own) * (v % 3) + own * (3 - 2 * at2 - late)
        return i, j

    def fill(dst, t, f, slot):
        for e in range(2):
            wide[slot, e, :, 0:LO * COLS] = histogram(f + e)
        one, two = wide[slot, 0], wide[slot, 1]
        lane = iota((HI, 128), 1)
        dst[t, 0:HI] = jnp.where(lane < LO * COLS, one, pltpu.roll(two, COLS, 1))
        below = jnp.concatenate([two[FOLD:HI], jnp.zeros((2 * FOLD - HI, 128), f32)], 0)
        dst[t, HI:HI + FOLD] = jnp.where(lane[0:FOLD] < 64, two[0:FOLD], pltpu.roll(below, 64, 1))

    def compute_sent(t, i, j, slot):
        fill(sent, t, feature(i, j, 1 - c), 2 * slot)

    def compute_kept(t, i, j, slot):
        fill(kept, t, feature(i, j, c), 2 * slot + 1)

    def step(turn, carry):
        for s in range(2):
            t = turn * 2 + s
            compute_sent(t, *place(t), s)
            compute_kept(t, *place(t), s)
        for s in range(2):
            core_copy(turn * 2 + s).start()

        @pl.when((turn > 0) & (turn < 5))
        def _():
            for s in range(2):
                t = turn * 2 - 2 + s
                finish(t)
                p1_copy(t, t, t % 3).start()

        @pl.when(turn == 5)
        def _():
            finish(8)
            p1_copy(8, 8, 2).start()
            finish(9)
            gather_plane(0)

        @pl.when(turn == 6)
        def _():
            finish(11)
            p1_copy(11, 9, 1).start()
            finish(10)
            gather_plane(1)

        for k, action in enumerate((leaves_0, leaves_1, leaves_2)):
            pl.when(turn == (1, 2, 4)[k])(action)
        return carry

    lax.fori_loop(0, 7, step, 0)
    compute_sent(14, 3, 0, 0)
    cross_copy().start()
    compute_kept(14, 3, 0, 0)
    p1_copy(14, 11, 0).start()
    compute_sent(15, 3, 3, 1)
    core_copy(15).start()
    finish(13)
    p1_copy(13, 10, 2).start()
    finish(12)
    gather_plane(2)
    compute_kept(15, 3, 3, 1)
    leaves_3()
    for i in range(3):
        p2_copy(i).wait_recv()
    for t, slot, j in ((11, 9, 1), (13, 10, 2), (14, 11, 0)):
        p1_copy(t, slot, j).wait_recv()
    cross_copy().wait_recv()

    hist = kept[15] + part2[0] + part2[1] + part2[2] + part1[9] + part1[10] + part1[11] + part1[12]
    core_copy(15).wait_recv()
    hist += mate[15]

    def split(x):
        a = x.astype(bf16)
        rest = x - a.astype(f32)
        b = rest.astype(bf16)
        return (rest - b.astype(f32)).astype(bf16), b, a

    def summed(pieces, ones):
        return sum(lax.dot_general(piece, ones, TN, preferred_element_type=f32) for piece in pieces)

    upper = split(jnp.concatenate([hist[0:HI], jnp.zeros((2 * FOLD - HI, 128), f32)], 0))
    folded = split(hist[HI:HI + FOLD])
    tops = [summed(upper, tri[k]) for k in range(LO)]
    first_half = [summed(folded, tri[k, 0:FOLD]) for k in range(2)]
    second_half = [summed(folded, tri[k, FOLD:2 * FOLD]) for k in range(2)]
    totals = (tops[0][0:32] + tops[1][32:64] + tops[2][64:96],
              first_half[0][0:32] + second_half[0][64:96] + first_half[1][32:64] + second_half[1][96:128] + tops[2][96:128])
    for e, total in enumerate(totals):
        g2, h2 = total[0:16], total[16:32]
        for grad_left, hess_left, out, stride in (
            (g2[0:8] + g2[8:16], h2[0:8] + h2[8:16], out1, 1), (g2, h2, out2, 2)):
            grad_total = grad_left[:, B - 1:B]
            hess_total = hess_left[:, B - 1:B]
            grad_right = grad_total - grad_left
            hess_right = hess_total - hess_left
            gain = (grad_left * grad_left / (hess_left + LAMBDA)
                    + grad_right * grad_right / (hess_right + LAMBDA)
                    - grad_total * grad_total / (hess_total + LAMBDA))
            for side in range(stride):
                for n in range(NODES1):
                    out[n * stride + side, e:e + 1, :] = gain[side * 8 + n:side * 8 + n + 1]

    for copy in stores[:2]:
        copy.start()
    for copy in route1 + route2 + leaf_copy(0) + leaf_copy(1) + leaf_copy(2):
        copy.wait_send()
    for t in list(range(14)) + [15]:
        core_copy(t).wait_send()
    for t in range(9):
        p1_copy(t, t, t % 3).wait_send()
    for t, slot, j in ((11, 9, 1), (13, 10, 2), (14, 11, 0)):
        p1_copy(t, slot, j).wait_send()
    cross_copy().wait_send()
    for i in range(3):
        p2_copy(i).wait_send()
    for copy in stores:
        copy.wait()


def copy_kernel(a, b, d, a_out, b_out, d_out):
    for src, dst in ((a, a_out), (b, b_out), (d, d_out)):
        dst[...] = src[...]


def hand_out(*arrays):
    return pl.pallas_call(
        copy_kernel,
        out_shape=tuple(jax.ShapeDtypeStruct(a.shape, a.dtype) for a in arrays),
        in_specs=[pl.BlockSpec(memory_space=pltpu.VMEM)] * 3,
        out_specs=[pl.BlockSpec(memory_space=pltpu.VMEM)] * 3,
        name="hand_out",
    )(*arrays)


def body(bins, grad, hess, margin, node_start, split_feat1, split_bin1, split_feat2, split_bin2):
    features, count = bins.shape
    lines = (count // 128, 128)
    own = features * 4 // 128
    dma = pltpu.SemaphoreType.DMA
    pair = (HI + FOLD, 128)
    gain1, gain2, new_margin = pl.pallas_call(
        kernel,
        out_shape=(
            jax.ShapeDtypeStruct((NODES1, own, B), f32),
            jax.ShapeDtypeStruct((NODES2, own, B), f32),
            jax.ShapeDtypeStruct(lines, f32)),
        in_specs=[pl.BlockSpec(memory_space=pltpu.HBM)] * 9,
        out_specs=[pl.BlockSpec(memory_space=pltpu.HBM)] * 3,
        scratch_shapes=[
            pltpu.VMEM((features, count), jnp.int32),
            pltpu.VMEM(lines, bf16),
            pltpu.VMEM(lines, bf16),
            pltpu.VMEM(lines, f32),
            pltpu.VMEM(lines, jnp.int32),
            pltpu.SMEM((NODES1,), jnp.int32),
            pltpu.SMEM((NODES1,), jnp.int32),
            pltpu.SMEM((NODES2,), jnp.int32),
            pltpu.SMEM((NODES2,), jnp.int32),
            pltpu.VMEM((NODES1, own, B), f32),
            pltpu.VMEM((NODES2, own, B), f32),
            pltpu.VMEM(lines, f32),
            pltpu.VMEM((4,) + lines, f32),
            pltpu.VMEM((NODES1, count), jnp.int32),
            dma((9,)), dma((3,)),
            pltpu.VMEM((features, count), f32),
            pltpu.VMEM((features, count), f32),
            pltpu.VMEM((COLS, count), bf16),
            pltpu.VMEM((NODES2, count), f32),
            pltpu.VMEM((2, 1, count), f32),
            pltpu.VMEM((16,) + pair, f32),
            pltpu.VMEM((16,) + pair, f32),
            pltpu.VMEM((16,) + pair, f32),
            pltpu.VMEM((13,) + pair, f32),
            pltpu.VMEM((3,) + pair, f32),
            pltpu.VMEM((3, COLS, 128), f32),
            pltpu.VMEM((LO, 2 * FOLD, B), bf16),
            pltpu.VMEM((4, 1, count), f32),
            pltpu.VMEM((4, 1, count), f32),
            pltpu.VMEM((COLS, 128), f32),
            pltpu.VMEM((3, COLS, 128), f32),
            pltpu.VMEM((3, COLS, 128), f32),
            pltpu.VMEM((4, 2, HI, 128), f32),
            dma((3,)), dma((3,)), dma((3,)), dma((3,)),
            dma((16,)), dma((16,)), dma((13,)), dma((13,)), dma((3,)), dma((3,)),
            dma((7,)), dma((7,)),
        ],
        compiler_params=pltpu.CompilerParams(
            collective_id=0, has_side_effects=True, vmem_limit_bytes=60 * 2**20),
        cost_estimate=pl.CostEstimate(flops=2 * 64 * 4096 * 8192, bytes_accessed=2**20, transcendentals=0),
    )(bins, grad.reshape(lines), hess.reshape(lines), margin.reshape(lines), node_start.reshape(lines),
      split_feat1, split_bin1, split_feat2, split_bin2)
    gain1, gain2, new_margin = hand_out(gain1, gain2, new_margin)
    return gain1, gain2, new_margin.reshape(count)


def solution(mesh):
    return jax.shard_map(
        body,
        mesh=mesh,
        in_specs=(P("feat", "row"), P("row"), P("row"), P("row"), P("row"), P(), P(), P(), P()),
        out_specs=(P(None, ("feat", "row"), None), P(None, ("feat", "row"), None), P("row")),
        check_vma=False,
    )
```
